256 devices in a mesh: ctx: 32 (over y, z), exp: 8 (over x, core).
Axes of the slice: x: 4, y: 4, z: 8, core: 2. Of those that a mesh axis runs over, the one named last changes fastest.
Arguments:
- hidden: bfloat16 [2048, 4096], P(('ctx', 'exp')), may hold values from -1.1953125 to 1.1953125
- queries: bfloat16 [2048, 4096], P('ctx', 'exp'), may hold values from -8 to 8
- keys: bfloat16 [2048, 256], P('ctx'), may hold values from -3 to 3
- values: bfloat16 [2048, 256], P('ctx'), may hold values from -6 to 6
- out_weight: bfloat16 [4096, 4096], P('exp', 'ctx'), may hold values from -0.09375 to 0.09375
- norm_gain: float32 [4096], replicated, may hold values from 0.5 to 1.5
- w_gate: bfloat16 [256, 4096, 384], P(('ctx', 'exp')), may hold values from -0.09375 to 0.09375
- w_up: bfloat16 [256, 4096, 384], P(('ctx', 'exp')), may hold values from -0.09375 to 0.09375
- w_down: bfloat16 [256, 384, 4096], P(('ctx', 'exp')), may hold values from -0.15625 to 0.15625
- routes: int32 [2048, 8], P(('ctx', 'exp')), may hold values from 0 to 63, all different within a row; in each aligned block of 8 rows (0 to 7, 8 to 15, ...) at most 2 rows name the same one
- gates: float32 [2048, 8], P(('ctx', 'exp')), may hold values from 0.05 to 0.5
Outputs:
- attended: bfloat16 [2048, 4096], P(('ctx', 'exp'))
- mixed: bfloat16 [2048, 4096], P(('ctx', 'exp'))
The draws below stay inside these ranges and needn't reach their ends.
Inputs may be any that keep to these rules, and one draw needn't show every extreme that they name: `routes`: each token names 8 different experts. In each aligned block of 8 rows (the rows of one device) no expert is named by more than 2 rows, and in some blocks one expert is named by exactly 2 rows.
All inputs are finite; a program needn't handle non-finite values.
Results may differ from the reference program's by a relative error of at most 0.025.
Values may be sent and summed in bfloat16 or wider, within the bound.
No kernel may reach another device: no remote copies, remote signals or barrier semaphores. Data moves between devices by JAX's collectives and lax.ppermute only.
A program may use at most 128 MiB of HBM per device.

```python
import math
import jax
import jax.numpy as jnp
import numpy as np
from jax import lax

D = 4096
HEAD_SIZE = 128
QUERY_HEADS = 32
KEY_VALUE_HEADS = 2
FF = 1536
PARTS_SIZE = 4
TOPK = 8
KEPT_TOKENS = 2048
ROWS_DEV = 8
FF_PART = 384
EXPERTS = 64
MOST = 2
CAPACITY = 512


def key_field(key):
    base_key = jax.random.fold_in(key, 11)
    layout_shape = (KEPT_TOKENS, KEY_VALUE_HEADS * HEAD_SIZE)
    bell_part = jnp.clip(jax.random.normal(base_key, layout_shape, jnp.float32), -3.0, 3.0)
    return bell_part


def draw_keys(key, part):
    sampled = key_field(key)
    return sampled.astype(jnp.bfloat16)


def draw_queries(key, part):
    entries = jnp.clip(2.0 * jax.random.normal(jax.random.fold_in(key, 23), (KEPT_TOKENS, QUERY_HEADS * HEAD_SIZE), jnp.float32), -8.0, 8.0)
    return entries.astype(jnp.bfloat16)


def block_scale(key, dims, shards, least, high):
    def one(axis_at, shards_of):
        steps = jax.random.uniform(jax.random.fold_in(jax.random.fold_in(key, 6), axis_at), (shards_of,), jnp.float32, least / len(shards), high / len(shards))
        return jnp.repeat(jnp.exp(steps), dims[axis_at] // shards_of).reshape((-1,) + (1,) * (len(dims) - axis_at - 1))

    loudness = one(*shards[0])
    for cut in shards[1:]:
        loudness = loudness * one(*cut)
    return loudness


def routed_block(key, own, number, rows, number_of, top, most, skew):
    sequence = jax.random.permutation(key, number_of)
    packed, common = portions_of(number_of, rows * top, most, skew, True), portions_of(number_of, rows * top, most, skew, False)
    places = jnp.arange(number_of)

    def named(tallies, offset_by):
        used = int((tallies > 0).sum())
        fixed = max(1, used // 4)
        passed = fixed + (places - fixed + offset_by * (used - fixed)) % max(1, number_of - fixed)
        return jnp.zeros((number_of,), jnp.int32).at[sequence[jnp.where(places < fixed, places, passed)]].set(jnp.asarray(tallies, jnp.int32))

    tallies = jnp.where(number % 4 == 0, named(packed, number // 4), named(common, number - number // 4 - 1))
    mixed = jax.random.permutation(jax.random.fold_in(own, 3), number_of)
    giver, receiver = mixed[0:number_of // 2 * 2:2], mixed[1:number_of // 2 * 2:2]
    room = jnp.minimum(tallies[giver] - 1, most - tallies[receiver]) // 2
    room = jnp.where((giver == sequence[0]) | (receiver == sequence[0]) | (tallies[receiver] == 0), 0, jnp.maximum(room, 0))
    passed = jax.random.randint(jax.random.fold_in(own, 4), (number_of // 2,), 0, 1 << 20) % (room + 1)
    tallies = tallies.at[giver].add(-passed).at[receiver].add(passed)
    members = jnp.searchsorted(jnp.cumsum(tallies), jnp.arange(rows * top), side="right").astype(jnp.int32)
    listing = members.reshape(top, rows).T
    listing = listing[jax.random.permutation(jax.random.fold_in(own, 1), rows)]
    offset_by = jax.random.randint(jax.random.fold_in(own, 2), (rows, 1), 0, top)
    return jnp.take_along_axis(listing, (jnp.arange(top)[None, :] + offset_by) % top, axis=1)


def portions_of(count, total, bound, lean, full):
    loads = [(1 << 20) // math.isqrt(grade ** lean) + 1 for grade in range(1, count + 1)]
    largest = bound if full else min(bound, max(-(-total // count), total * loads[0] // sum(loads)))
    least = 1 if total - largest >= count - 1 else 0
    counts, rest = [largest] + [least] * (count - 1), total - largest - least * (count - 1)
    while rest > 0:
        free = [i for i in range(1, count) if counts[i] < largest] or [i for i in range(1, count) if counts[i] < bound]
        mass, budget = sum([loads[i] for i in free]), rest
        for i in free:
            extra = min(bound - counts[i], max(1, budget * loads[i] // mass), rest)
            counts[i] = counts[i] + extra
            rest = rest - extra
    return np.array(counts)


def normal_values(stream_key, dims, deviation, reach, cuts=(), held_as=jnp.bfloat16):
    factor_of = block_scale(stream_key, dims, cuts, -0.22, 0.18) if cuts else 1.0
    values = jax.random.normal(stream_key, dims, jnp.float32) * deviation * factor_of
    return jnp.minimum(jnp.maximum(values, -reach), reach).astype(held_as)


def setup_inputs(seed: int = 0) -> dict:
    key_list = jax.random.split(jax.random.key(seed), 12)
    hidden = normal_values(key_list[0], (KEPT_TOKENS, D), 0.2, 1.1953125, ((0, 256),))
    queries = draw_queries(jax.random.fold_in(key_list[11], 71), 0)
    keys = draw_keys(jax.random.fold_in(key_list[11], 71), 0)
    values = normal_values(key_list[3], (KEPT_TOKENS, KEY_VALUE_HEADS * HEAD_SIZE), 1.0, 6.0, ((0, 32),))
    out_weight = normal_values(key_list[4], (QUERY_HEADS * HEAD_SIZE, D), (QUERY_HEADS * HEAD_SIZE) ** -0.5, 0.09375, ((0, 8), (1, 32)))
    norm_gain = jnp.clip(1.0 + 0.1 * jax.random.normal(key_list[5], (D,), jnp.float32), 0.5, 1.5)
    w_gate = normal_values(key_list[6], (PARTS_SIZE * EXPERTS, D, FF_PART), D ** -0.5, 0.09375, ((0, 256),))
    w_up = normal_values(key_list[7], (PARTS_SIZE * EXPERTS, D, FF_PART), D ** -0.5, 0.09375, ((0, 256),))
    w_down = normal_values(key_list[8], (PARTS_SIZE * EXPERTS, FF_PART, D), FF ** -0.5, 0.15625, ((0, 256),))
    routes_keys = jax.random.split(jax.random.fold_in(key_list[9], 1), KEPT_TOKENS // ROWS_DEV)
    routes_turns = jax.random.permutation(jax.random.fold_in(key_list[9], 3), KEPT_TOKENS // ROWS_DEV)
    routes = jax.vmap(lambda own, number: routed_block(jax.random.fold_in(key_list[9], 2), own, number, ROWS_DEV, EXPERTS, TOPK, MOST, 2))(routes_keys, routes_turns).reshape((KEPT_TOKENS, TOPK))
    gates = jnp.clip(jnp.exp(math.log(0.5) - 2.3025851 * jax.random.uniform(key_list[10], (KEPT_TOKENS, TOPK), jnp.float32) ** block_scale(key_list[10], (KEPT_TOKENS, TOPK), ((0, 256),), -0.2, 0.2)), 0.05, 0.5)
    return {"hidden": hidden, "queries": queries, "keys": keys, "values": values, "out_weight": out_weight, "norm_gain": norm_gain, "w_gate": w_gate, "w_up": w_up, "w_down": w_down, "routes": routes, "gates": gates}


def attend_rows(queries, keys, values, row_shift, rows_per_block):
    queries_per_group = QUERY_HEADS // KEY_VALUE_HEADS
    block_queries = lax.dynamic_slice_in_dim(queries, row_shift, rows_per_block, 0).astype(jnp.float32).reshape(rows_per_block, KEY_VALUE_HEADS, queries_per_group, HEAD_SIZE)
    every_key = keys.astype(jnp.float32).reshape(KEPT_TOKENS, KEY_VALUE_HEADS, HEAD_SIZE)
    every_value = values.astype(jnp.float32).reshape(KEPT_TOKENS, KEY_VALUE_HEADS, HEAD_SIZE)
    scores = jnp.einsum('qgjd,kgd->gjqk', block_queries, every_key) * HEAD_SIZE ** (-0.5)
    query_pos = row_shift + jnp.arange(rows_per_block, dtype=jnp.int32)
    key_pos = jnp.arange(KEPT_TOKENS, dtype=jnp.int32)
    visible = key_pos[None, :] <= query_pos[:, None]
    scores = jnp.where(visible, scores, -1e+30)
    highest = lax.optimization_barrier(jnp.max(scores, axis=-1, keepdims=True))
    probs = jnp.where(visible, jnp.exp(scores - highest), 0.0)
    denom = lax.optimization_barrier(jnp.sum(probs, axis=-1))
    rounded = lax.optimization_barrier(probs.astype(jnp.bfloat16)).astype(jnp.float32)
    weighted = jnp.einsum('gjqk,kgd->qgjd', rounded, every_value)
    result = weighted / jnp.transpose(denom, (2, 0, 1))[..., None]
    return result.reshape(rows_per_block, QUERY_HEADS * HEAD_SIZE).astype(jnp.bfloat16)

def reference(hidden, queries, keys, values, out_weight, norm_gain, w_gate, w_up, w_down, routes, gates):
    rows_per_block = min(512, KEPT_TOKENS)
    starts = jnp.arange(KEPT_TOKENS // rows_per_block, dtype=jnp.int32) * rows_per_block

    def one_block(row_shift):
        return attend_rows(queries, keys, values, row_shift, rows_per_block)
    attention = lax.map(one_block, starts).reshape(KEPT_TOKENS, QUERY_HEADS * HEAD_SIZE)
    residual = hidden.astype(jnp.float32) + jnp.dot(attention, out_weight, preferred_element_type=jnp.float32)
    attended = residual.astype(jnp.bfloat16)
    mean_square = lax.optimization_barrier(jnp.mean(residual * residual, axis=-1, keepdims=True))
    normed = (residual * lax.rsqrt(mean_square + 1e-06) * norm_gain).astype(jnp.bfloat16)

    def expert_step(running, expert):
        matches = routes == expert
        row_hit = jnp.any(matches, axis=1)
        row_gate = lax.optimization_barrier(jnp.sum(jnp.where(matches, gates, 0.0), axis=1))
        picked = jnp.nonzero(row_hit, size=CAPACITY, fill_value=0)[0].astype(jnp.int32)
        filled = jnp.arange(CAPACITY, dtype=jnp.int32) < jnp.sum(row_hit.astype(jnp.int32))
        chosen = normed[picked]
        summed = jnp.zeros((CAPACITY, D), jnp.float32)
        for part_index in range(PARTS_SIZE):
            slice_index = part_index * EXPERTS + expert
            gate_h = jnp.dot(chosen, w_gate[slice_index], preferred_element_type=jnp.float32)
            up_h = jnp.dot(chosen, w_up[slice_index], preferred_element_type=jnp.float32)
            inner = (jax.nn.silu(gate_h) * up_h).astype(jnp.bfloat16)
            part_out = jnp.dot(inner, w_down[slice_index], preferred_element_type=jnp.float32).astype(jnp.bfloat16)
            summed = summed + lax.optimization_barrier(part_out).astype(jnp.float32)
        weight = jnp.where(filled, row_gate[picked], 0.0)
        running = running.at[picked].add(summed * weight[:, None])
        return (running, None)
    expert_ids = jnp.arange(EXPERTS, dtype=jnp.int32)
    moe, unused = lax.scan(expert_step, jnp.zeros((KEPT_TOKENS, D), jnp.float32), expert_ids)
    mixed = (residual + moe).astype(jnp.bfloat16)
    return (attended, mixed)
```

```python
import jax
import jax.numpy as jnp
from jax import lax
from jax.sharding import Mesh
from jax.sharding import PartitionSpec as P

D = 4096
HEAD_SIZE = 128
QUERY_HEADS = 32
KEY_VALUE_HEADS = 2
TOPK = 8
MOST = 2
Y, Z, X, CORE = 4, 8, 4, 2
CTX = ("y", "z")
EXP = ("x", "core")
LANES = X * CORE
BF16 = jnp.bfloat16
F32 = jnp.float32


def spread(block, axes, count):
    return lax.all_to_all(
        jnp.broadcast_to(block[None], (count,) + block.shape), axes, 0, 0, tiled=True
    )


def swap(blocks, axes):
    return lax.all_to_all(blocks, axes, 0, 0, tiled=True)


def shift(block, step):
    return lax.ppermute(block, "y", [(i, (i + step) % Y) for i in range(Y)])


def on_device(
    hidden, queries, keys, values, out_weight, norm_gain, w_gate, w_up, w_down, routes, gates
):
    rows_ctx = queries.shape[0]
    heads = queries.shape[1] // HEAD_SIZE
    rows = routes.shape[0]
    lane = lax.axis_index(EXP)
    ctx = lax.axis_index(CTX)
    group = lax.axis_index("z")
    scale = HEAD_SIZE ** (-0.5)

    weight_piece = lax.all_gather(out_weight, "z", axis=0, tiled=False)

    table = jnp.concatenate([routes.astype(F32), gates], axis=1)
    table = spread(table, "z", Z).reshape(Z, rows, 2 * TOPK)
    routes_z = table[..., :TOPK].astype(jnp.int32)
    gates_z = table[..., TOPK:]
    own = group * LANES + jnp.arange(LANES, dtype=jnp.int32)
    named = routes_z[:, :, :, None] == own
    hit = jnp.any(named, axis=2)
    gate = jnp.sum(jnp.where(named, gates_z[..., None], 0.0), axis=2)
    earlier = jnp.cumsum(hit.astype(jnp.int32), axis=1) - hit.astype(jnp.int32)
    slots = jnp.arange(MOST, dtype=jnp.int32)
    chosen = hit[..., None] & (earlier[..., None] == slots)
    same = jnp.eye(Z, dtype=bool)
    pick = chosen.transpose(2, 0, 3, 1)[:, :, :, None, :] & same[None, :, None, :, None]
    pick = pick.reshape(LANES * Z * MOST, Z * rows)
    place = jnp.where(
        chosen.transpose(0, 1, 2, 3)[:, :, :, None, :] & same[:, None, None, :, None],
        gate[:, :, :, None, None],
        0.0,
    ).reshape(Z * rows, LANES * Z * MOST)
    place_high = place.astype(BF16)
    place_low = (place - place_high.astype(F32)).astype(BF16)

    head = lane * heads // (QUERY_HEADS // KEY_VALUE_HEADS)
    key_head = lax.dynamic_slice_in_dim(keys, head * HEAD_SIZE, HEAD_SIZE, 1)
    value_head = lax.dynamic_slice_in_dim(values, head * HEAD_SIZE, HEAD_SIZE, 1)
    both = spread(jnp.concatenate([key_head, value_head], axis=1), CTX, Y * Z)
    both = both.reshape(Y * Z * rows_ctx, 2 * HEAD_SIZE)
    key_piece, value_piece = both[:, :HEAD_SIZE], both[:, HEAD_SIZE:]
    query_rows = queries.reshape(rows_ctx, heads, HEAD_SIZE)
    query_pos = ctx * rows_ctx + jnp.arange(rows_ctx, dtype=jnp.int32)
    scores = jnp.einsum("qhd,kd->qhk", query_rows, key_piece, preferred_element_type=F32) * scale
    key_pos = jnp.arange(key_piece.shape[0], dtype=jnp.int32)
    visible = (key_pos[None, :] <= query_pos[:, None])[:, None, :]
    scores = jnp.where(visible, scores, -1e30)
    peak = jnp.max(scores, axis=-1)
    weights = jnp.where(visible, jnp.exp(scores - peak[..., None]), 0.0)
    totals = jnp.sum(weights, axis=-1)
    accumulated = jnp.einsum(
        "qhk,kd->qhd", weights.astype(BF16), value_piece, preferred_element_type=F32
    )
    attention = (
        (accumulated / totals[..., None]).reshape(rows_ctx, heads * HEAD_SIZE).astype(BF16)
    )

    attention_y = spread(attention, "y", Y).reshape(Y * rows_ctx, heads * HEAD_SIZE)
    partial = jnp.einsum("rf,zfc->rzc", attention_y, weight_piece, preferred_element_type=F32)
    width = D // Y
    partial = partial.astype(BF16).reshape(Y, LANES, rows, width).transpose(1, 0, 2, 3)
    summed = jnp.sum(swap(partial, EXP).astype(F32), axis=0).astype(BF16)
    projected = swap(summed, "y").transpose(1, 0, 2).reshape(rows, D)
    residual = hidden.astype(F32) + projected.astype(F32)
    attended = residual.astype(BF16)
    mean_square = jnp.mean(residual * residual, axis=-1, keepdims=True)
    normed = (residual * lax.rsqrt(mean_square + 1e-06) * norm_gain).astype(BF16)

    normed_z = spread(normed, "z", Z).reshape(Z * rows, D)
    outbox = jnp.dot(pick.astype(BF16), normed_z, preferred_element_type=F32).astype(BF16)
    inbox = swap(outbox.reshape(LANES, Z * MOST, D), EXP).reshape(LANES * Z * MOST, D)
    half = inbox.shape[0] // 2
    before = shift(inbox, 1)
    after = shift(inbox, -1)
    across = jnp.concatenate([shift(after[:half], -1), shift(before[half:], 1)], axis=0)

    def expert(block):
        gate_h = jnp.dot(block, w_gate[0], preferred_element_type=F32)
        up_h = jnp.dot(block, w_up[0], preferred_element_type=F32)
        inner = (jax.nn.silu(gate_h) * up_h).astype(BF16)
        return jnp.dot(inner, w_down[0], preferred_element_type=F32).astype(BF16)

    out_own = expert(inbox)
    out_near = expert(jnp.concatenate([before, after], axis=0))
    out_before, out_after = out_near[: 2 * half], out_near[2 * half :]
    out_across = expert(across)

    far_after = shift(out_across[:half], 1)
    far_before = shift(out_across[half:], -1)
    to_after = jnp.concatenate(
        [
            (out_after[:half].astype(F32) + far_after.astype(F32)).astype(BF16),
            out_after[half:],
        ],
        axis=0,
    )
    to_before = jnp.concatenate(
        [
            out_before[:half],
            (out_before[half:].astype(F32) + far_before.astype(F32)).astype(BF16),
        ],
        axis=0,
    )
    returned = (
        out_own.astype(F32) + shift(to_after, 1).astype(F32) + shift(to_before, -1).astype(F32)
    ).astype(BF16)
    back = swap(returned.reshape(LANES, Z * MOST, D), EXP).reshape(LANES * Z * MOST, D)
    moe_z = jnp.dot(place_high, back, preferred_element_type=F32) + jnp.dot(
        place_low, back, preferred_element_type=F32
    )
    moe = jnp.sum(swap(moe_z.astype(BF16).reshape(Z, rows, D), "z").astype(F32), axis=0)
    mixed = (residual + moe).astype(BF16)
    return (attended, mixed)


def solution(mesh):
    fine = Mesh(mesh.devices.reshape(Y, Z, X, CORE), CTX + EXP)
    every = CTX + EXP
    return jax.shard_map(
        on_device,
        mesh=fine,
        in_specs=(
            P(every, None),
            P(CTX, EXP),
            P(CTX, None),
            P(CTX, None),
            P(EXP, CTX),
            P(),
            P(every, None, None),
            P(every, None, None),
            P(every, None, None),
            P(every, None),
            P(every, None),
        ),
        out_specs=(P(every, None), P(every, None)),
        check_vma=False,
    )
```

```python
import jax
import jax.numpy as jnp
from jax import lax
from jax.sharding import Mesh
from jax.sharding import PartitionSpec as P

D = 4096
HEAD_SIZE = 128
QUERY_HEADS = 32
KEY_VALUE_HEADS = 2
TOPK = 8
MOST = 2
Y, Z, X, CORE = 4, 8, 4, 2
CTX = ("y", "z")
EXP = ("x", "core")
LANES = X * CORE
BF16 = jnp.bfloat16
F32 = jnp.float32


def spread(block, axes, count):
    return lax.all_to_all(
        jnp.broadcast_to(block[None], (count,) + block.shape), axes, 0, 0, tiled=True
    )


def swap(blocks, axes):
    return lax.all_to_all(blocks, axes, 0, 0, tiled=True)


def shift(block, step):
    return lax.ppermute(block, "y", [(i, (i + step) % Y) for i in range(Y)])


def slots_of(routes):
    experts = jnp.arange(Z * LANES, dtype=jnp.int32)
    named = routes[..., None] == experts
    hit = jnp.any(named, axis=-2)
    count = hit.astype(jnp.int32)
    earlier = jnp.cumsum(count, axis=-2) - count
    chosen = hit[..., None] & (earlier[..., None] == jnp.arange(MOST, dtype=jnp.int32))
    return chosen, named


def on_device(
    hidden, queries, keys, values, out_weight, norm_gain, w_gate, w_up, w_down, routes, gates
):
    rows_ctx = queries.shape[0]
    heads = queries.shape[1] // HEAD_SIZE
    rows = routes.shape[0]
    piece = D // Z
    lane = lax.axis_index(EXP)
    ctx = lax.axis_index(CTX)
    core = lax.axis_index("core")
    scale = HEAD_SIZE ** (-0.5)

    weight_y = lax.all_gather(out_weight, "y", axis=0, tiled=False)
    weight_y = weight_y.transpose(1, 0, 2).reshape(out_weight.shape[0], piece)

    head = lane * heads // (QUERY_HEADS // KEY_VALUE_HEADS)
    half_ctx = rows_ctx // CORE
    key_head = lax.dynamic_slice(keys, (core * half_ctx, head * HEAD_SIZE), (half_ctx, HEAD_SIZE))
    value_head = lax.dynamic_slice(
        values, (core * half_ctx, head * HEAD_SIZE), (half_ctx, HEAD_SIZE)
    )
    mine = spread(jnp.concatenate([key_head, value_head], axis=1), CTX, Y * Z)
    mine = mine.reshape(Y * Z * half_ctx, 2 * HEAD_SIZE)
    other = lax.ppermute(mine, "core", [(0, 1), (1, 0)])
    query_rows = queries.reshape(rows_ctx * heads, HEAD_SIZE)
    query_pos = ctx * rows_ctx + jnp.arange(rows_ctx * heads, dtype=jnp.int32) // heads
    index = jnp.arange(Y * Z * half_ctx, dtype=jnp.int32)
    base_pos = (index // half_ctx) * rows_ctx + index % half_ctx
    scored = []
    for both, part in ((mine, core), (other, 1 - core)):
        scores = (
            jnp.einsum(
                "qd,kd->qk", query_rows, both[:, :HEAD_SIZE], preferred_element_type=F32
            )
            * scale
        )
        visible = (base_pos + part * half_ctx)[None, :] <= query_pos[:, None]
        scored.append((jnp.where(visible, scores, -1e30), visible, both[:, HEAD_SIZE:]))
    peak = jnp.maximum(jnp.max(scored[0][0], axis=-1), jnp.max(scored[1][0], axis=-1))
    totals, accumulated = 0.0, 0.0
    for scores, visible, value_piece in scored:
        weights = jnp.where(visible, jnp.exp(scores - peak[:, None]), 0.0)
        totals = totals + jnp.sum(weights, axis=-1)
        accumulated = accumulated + jnp.dot(
            weights.astype(BF16), value_piece, preferred_element_type=F32
        )
    attention = (
        (accumulated / totals[:, None]).reshape(rows_ctx, heads * HEAD_SIZE).astype(BF16)
    )

    hidden_z = hidden.reshape(rows, Y, Z, HEAD_SIZE).transpose(2, 0, 1, 3).reshape(Z, rows, piece)
    routes_wide = jnp.pad(routes.astype(BF16), ((0, 0), (0, piece - TOPK)))
    parcel = jnp.concatenate(
        [
            jnp.broadcast_to(attention[None], (Z, rows_ctx, piece)),
            hidden_z,
            jnp.broadcast_to(routes_wide[None], (Z, rows, piece)),
        ],
        axis=1,
    )
    parcel = swap(parcel, "z")
    attention_z = parcel[:, :rows_ctx].reshape(Z, LANES, rows, piece)
    hidden_c = parcel[:, rows_ctx : rows_ctx + rows].astype(F32)
    routes_c = parcel[:, rows_ctx + rows :, :TOPK].astype(jnp.int32)

    partial = jnp.einsum("zerf,fc->ezrc", attention_z, weight_y, preferred_element_type=F32)
    projected_c = jnp.sum(swap(partial.astype(BF16), EXP).astype(F32), axis=0)
    residual_c = (hidden_c + projected_c).astype(BF16).reshape(Z * rows, piece)

    chosen, _ = slots_of(routes_c)
    same = jnp.eye(Z, dtype=bool)
    pick = chosen.transpose(2, 0, 3, 1)[:, :, :, None, :] & same[None, :, None, :, None]
    pick = pick.reshape(Z * LANES * Z * MOST, Z * rows).astype(BF16)
    outbox = jnp.dot(pick, residual_c, preferred_element_type=F32).astype(BF16)
    inbox = swap(outbox.reshape(Z * LANES, Z * MOST, piece), ("z",) + EXP)
    inbox, projected_c = lax.optimization_barrier((inbox, projected_c.astype(BF16)))
    slots = LANES * Z * MOST
    inbox = inbox.reshape(Z, slots, Y, HEAD_SIZE).transpose(1, 2, 0, 3).reshape(slots, D)
    inbox = inbox.astype(F32)
    mean_square = jnp.mean(inbox * inbox, axis=-1, keepdims=True)
    inbox = (inbox * lax.rsqrt(mean_square + 1e-06) * norm_gain).astype(BF16)

    half = slots // 2
    before = shift(inbox, 1)
    after = shift(inbox, -1)
    across_low = shift(after[:half], -1)
    across_high = shift(before[half:], 1)

    projected = swap(projected_c, "z").reshape(Z, rows, Y, HEAD_SIZE)
    projected = projected.transpose(1, 2, 0, 3).reshape(rows, D)
    residual = hidden.astype(F32) + projected.astype(F32)
    attended = residual.astype(BF16)

    def expert(block):
        block, gate_w, up_w, down_w = lax.optimization_barrier(
            (block, w_gate[0], w_up[0], w_down[0])
        )
        gate_h = jnp.dot(block, gate_w, preferred_element_type=F32)
        up_h = jnp.dot(block, up_w, preferred_element_type=F32)
        inner = (jax.nn.silu(gate_h) * up_h).astype(BF16)
        return jnp.dot(inner, down_w, preferred_element_type=F32).astype(BF16)

    out_own = expert(inbox)
    out_before = expert(before)
    out_after = expert(after)
    home_low = shift(out_before[:half], -1)
    home_high = shift(out_after[half:], 1)
    out_across = expert(jnp.concatenate([across_low, across_high], axis=0))
    far_after = shift(out_across[:half], 1)
    far_before = shift(out_across[half:], -1)
    sum_low = shift((out_after[:half].astype(F32) + far_after.astype(F32)).astype(BF16), 1)
    sum_high = shift((out_before[half:].astype(F32) + far_before.astype(F32)).astype(BF16), -1)
    low = out_own[:half].astype(F32) + home_low.astype(F32) + sum_low.astype(F32)
    high = out_own[half:].astype(F32) + home_high.astype(F32) + sum_high.astype(F32)
    returned = jnp.concatenate([low.astype(BF16), high.astype(BF16)], axis=0)

    back = swap(returned.reshape(LANES * Z, MOST, D), EXP + ("z",)).reshape(slots, D)
    chosen_own, named = slots_of(routes)
    gate = jnp.sum(jnp.where(named, gates[..., None], 0.0), axis=1)
    place = jnp.where(chosen_own, gate[..., None], 0.0).reshape(rows, Z, LANES, MOST)
    place = place.transpose(0, 2, 1, 3).reshape(rows, slots)
    place_high = place.astype(BF16)
    place_low = (place - place_high.astype(F32)).astype(BF16)
    moe = jnp.dot(place_high, back, preferred_element_type=F32) + jnp.dot(
        place_low, back, preferred_element_type=F32
    )
    mixed = (residual + moe).astype(BF16)
    return (attended, mixed)


def solution(mesh):
    fine = Mesh(mesh.devices.reshape(Y, Z, X, CORE), CTX + EXP)
    every = CTX + EXP
    return jax.shard_map(
        on_device,
        mesh=fine,
        in_specs=(
            P(every, None),
            P(CTX, EXP),
            P(CTX, None),
            P(CTX, None),
            P(EXP, CTX),
            P(),
            P(every, None, None),
            P(every, None, None),
            P(every, None, None),
            P(every, None),
            P(every, None),
        ),
        out_specs=(P(every, None), P(every, None)),
        check_vma=False,
    )
```

```python
import jax
import jax.numpy as jnp
from jax import lax
from jax.experimental import pallas as pl
from jax.experimental.pallas import tpu as pltpu
from jax.sharding import Mesh
from jax.sharding import PartitionSpec as P

D = 4096
HEAD_SIZE = 128
QUERY_HEADS = 32
KEY_VALUE_HEADS = 2
TOPK = 8
MOST = 2
Y, Z, X, CORE = 4, 8, 4, 2
CTX = ("y", "z")
EXP = ("x", "core")
LANES = X * CORE
BF16 = jnp.bfloat16
F32 = jnp.float32


def spread(block, axes, count):
    return lax.all_to_all(
        jnp.broadcast_to(block[None], (count,) + block.shape), axes, 0, 0, tiled=True
    )


def swap(blocks, axes):
    return lax.all_to_all(blocks, axes, 0, 0, tiled=True)


def shift(block, step):
    return lax.ppermute(block, "y", [(i, (i + step) % Y) for i in range(Y)])


def norm_kernel(x_ref, gain_ref, low_ref, high_ref):
    lanes = LANES // 2
    rows, piece = lanes * x_ref.shape[1], x_ref.shape[2]
    for part, out_ref in enumerate((low_ref, high_ref)):

        def piece_of(i):
            x = x_ref[i * LANES + part * lanes : i * LANES + (part + 1) * lanes]
            return x.reshape(rows, piece).astype(F32)

        square = jnp.zeros((rows, 1), F32)
        for i in range(Z):
            x = piece_of(i)
            square = square + jnp.sum(x * x, axis=-1, keepdims=True)
        factor = lax.rsqrt(square * (1.0 / D) + 1e-06)
        for i in range(Z):
            x = piece_of(i) * factor
            for j in range(Y):
                at = (j * Z + i) * HEAD_SIZE
                out_ref[:, at : at + HEAD_SIZE] = (
                    x[:, j * HEAD_SIZE : (j + 1) * HEAD_SIZE] * gain_ref[:, at : at + HEAD_SIZE]
                ).astype(BF16)


def normalise(inbox, gain):
    rows = inbox.shape[0] * inbox.shape[1] // Z // 2
    return pl.pallas_call(
        norm_kernel,
        out_shape=[jax.ShapeDtypeStruct((rows, D), BF16)] * 2,
        in_specs=[pl.BlockSpec(memory_space=pltpu.VMEM)] * 2,
        out_specs=[pl.BlockSpec(memory_space=pltpu.VMEM)] * 2,
        compiler_params=pltpu.CompilerParams(vmem_limit_bytes=32 * 1024 * 1024),
        cost_estimate=pl.CostEstimate(flops=6 * rows * D, bytes_accessed=8 * rows * D, transcendentals=0),
    )(inbox, gain.reshape(1, D))


STEPS = 4


def expert_kernel(
    low_ref, high_ref, gate_ref, up_ref, down_ref, out_low_ref, out_high_ref, gate_sum, up_sum, inner
):
    step = pl.program_id(0)
    depth = gate_ref.shape[0]
    rows = low_ref.shape[0]

    @pl.when(step < STEPS)
    def _():
        columns = pl.ds(pl.multiple_of(step * depth, depth), depth)
        x = jnp.concatenate([low_ref[:, columns], high_ref[:, columns]], axis=0)
        gate_h = jnp.dot(x, gate_ref[...], preferred_element_type=F32)
        up_h = jnp.dot(x, up_ref[...], preferred_element_type=F32)

        @pl.when(step == 0)
        def _():
            gate_sum[...] = gate_h
            up_sum[...] = up_h

        @pl.when(step > 0)
        def _():
            gate_sum[...] += gate_h
            up_sum[...] += up_h

    @pl.when(step == STEPS - 1)
    def _():
        v = gate_sum[...]
        inner[...] = (v / (1.0 + jnp.exp(-v)) * up_sum[...]).astype(BF16)

    @pl.when(step >= STEPS)
    def _():
        out = jnp.dot(inner[...], down_ref[...], preferred_element_type=F32).astype(BF16)
        out_low_ref[...] = out[:rows]
        out_high_ref[...] = out[rows:]


def expert(low, high, w_gate, w_up, w_down):
    rows = low.shape[0]
    width = w_gate.shape[1]
    piece = D // STEPS
    whole = pl.BlockSpec((rows, D), lambda i: (0, 0))
    into = pl.BlockSpec((piece, width), lambda i: (jnp.minimum(i, STEPS - 1), 0))
    out_of = pl.BlockSpec((width, piece), lambda i: (0, jnp.maximum(i - STEPS, 0)))
    result = pl.BlockSpec((rows, piece), lambda i: (0, jnp.maximum(i - STEPS, 0)))
    return pl.pallas_call(
        expert_kernel,
        grid=(2 * STEPS,),
        out_shape=[jax.ShapeDtypeStruct((rows, D), BF16)] * 2,
        in_specs=[whole, whole, into, into, out_of],
        out_specs=[result, result],
        scratch_shapes=[
            pltpu.VMEM((2 * rows, width), F32),
            pltpu.VMEM((2 * rows, width), F32),
            pltpu.VMEM((2 * rows, width), BF16),
        ],
        compiler_params=pltpu.CompilerParams(
            dimension_semantics=("arbitrary",), vmem_limit_bytes=32 * 1024 * 1024
        ),
        cost_estimate=pl.CostEstimate(
            flops=12 * rows * D * width,
            bytes_accessed=6 * D * width + 8 * rows * D,
            transcendentals=2 * rows * width,
        ),
    )(low, high, w_gate, w_up, w_down)


def slots_of(routes):
    experts = jnp.arange(Z * LANES, dtype=jnp.int32)
    named = routes[..., None] == experts
    hit = jnp.any(named, axis=-2)
    count = hit.astype(jnp.int32)
    earlier = jnp.cumsum(count, axis=-2) - count
    chosen = hit[..., None] & (earlier[..., None] == jnp.arange(MOST, dtype=jnp.int32))
    return chosen, named


def on_device(
    hidden, queries, keys, values, out_weight, norm_gain, w_gate, w_up, w_down, routes, gates
):
    rows_ctx = queries.shape[0]
    heads = queries.shape[1] // HEAD_SIZE
    rows = routes.shape[0]
    piece = D // Z
    lane = lax.axis_index(EXP)
    ctx = lax.axis_index(CTX)
    core = lax.axis_index("core")
    scale = HEAD_SIZE ** (-0.5)

    pieces = [out_weight] + [shift(out_weight, step) for step in range(1, Y)]
    by_distance = jnp.stack(pieces[::-1] * 2)
    weight_y = lax.dynamic_slice_in_dim(by_distance, Y - 1 - lax.axis_index("y"), Y, 0)
    weight_y = weight_y.transpose(1, 0, 2).reshape(out_weight.shape[0], piece)

    head = lane * heads // (QUERY_HEADS // KEY_VALUE_HEADS)
    half_ctx = rows_ctx // CORE
    key_head = lax.dynamic_slice(keys, (core * half_ctx, head * HEAD_SIZE), (half_ctx, HEAD_SIZE))
    value_head = lax.dynamic_slice(
        values, (core * half_ctx, head * HEAD_SIZE), (half_ctx, HEAD_SIZE)
    )
    mine = spread(jnp.concatenate([key_head, value_head], axis=1), CTX, Y * Z)
    mine = mine.reshape(Y * Z * half_ctx, 2 * HEAD_SIZE)
    other = lax.ppermute(mine, "core", [(0, 1), (1, 0)])
    query_rows = queries.reshape(rows_ctx * heads, HEAD_SIZE)
    query_pos = ctx * rows_ctx + jnp.arange(rows_ctx * heads, dtype=jnp.int32) // heads
    index = jnp.arange(Y * Z * half_ctx, dtype=jnp.int32)
    base_pos = (index // half_ctx) * rows_ctx + index % half_ctx
    scored = []
    for both, part in ((mine, core), (other, 1 - core)):
        scores = (
            jnp.einsum(
                "qd,kd->qk", query_rows, both[:, :HEAD_SIZE], preferred_element_type=F32
            )
            * scale
        )
        visible = (base_pos + part * half_ctx)[None, :] <= query_pos[:, None]
        scored.append((jnp.where(visible, scores, -1e30), visible, both[:, HEAD_SIZE:]))
    peak = jnp.maximum(jnp.max(scored[0][0], axis=-1), jnp.max(scored[1][0], axis=-1))
    totals, accumulated = 0.0, 0.0
    for scores, visible, value_piece in scored:
        weights = jnp.where(visible, jnp.exp(scores - peak[:, None]), 0.0)
        totals = totals + jnp.sum(weights, axis=-1)
        accumulated = accumulated + jnp.dot(
            weights.astype(BF16), value_piece, preferred_element_type=F32
        )
    attention = (
        (accumulated / totals[:, None]).reshape(rows_ctx, heads * HEAD_SIZE).astype(BF16)
    )

    hidden_z = hidden.reshape(rows, Y, Z, HEAD_SIZE).transpose(2, 0, 1, 3).reshape(Z, rows, piece)
    gates_high = gates.astype(BF16)
    gates_rest = gates - gates_high.astype(F32)
    gates_mid = gates_rest.astype(BF16)
    gates_low = (gates_rest - gates_mid.astype(F32)).astype(BF16)
    table = jnp.concatenate([routes.astype(BF16), gates_high, gates_mid, gates_low], axis=1)
    table = jnp.pad(table, ((0, 0), (0, piece - table.shape[1])))
    parcel = jnp.concatenate(
        [
            jnp.broadcast_to(attention[None], (Z, rows_ctx, piece)),
            hidden_z,
            jnp.broadcast_to(table[None], (Z, rows, piece)),
        ],
        axis=1,
    )
    parcel = swap(parcel, "z")
    attention_z = parcel[:, :rows_ctx].reshape(Z, LANES, rows, piece)
    hidden_c = parcel[:, rows_ctx : rows_ctx + rows].astype(F32)
    table_c = parcel[:, rows_ctx + rows :, : 4 * TOPK].astype(F32).reshape(Z, rows, 4, TOPK)
    routes_c = table_c[:, :, 0].astype(jnp.int32)
    gates_c = table_c[:, :, 1] + table_c[:, :, 2] + table_c[:, :, 3]

    partial = jnp.einsum("zerf,fc->ezrc", attention_z, weight_y, preferred_element_type=F32)
    projected_c = jnp.sum(swap(partial.astype(BF16), EXP).astype(F32), axis=0)
    residual_c = (hidden_c + projected_c).astype(BF16).reshape(Z * rows, piece)

    chosen, named = slots_of(routes_c)
    same = jnp.eye(Z, dtype=bool)
    pick = chosen.transpose(2, 0, 3, 1)[:, :, :, None, :] & same[None, :, None, :, None]
    pick = pick.reshape(Z * LANES * Z * MOST, Z * rows).astype(BF16)
    outbox = jnp.dot(pick, residual_c, preferred_element_type=F32).astype(BF16)
    inbox = swap(outbox.reshape(Z * LANES, Z * MOST, piece), ("z",) + EXP)
    inbox, projected_c = lax.optimization_barrier((inbox, projected_c.astype(BF16)))
    slots = LANES * Z * MOST
    low, high = normalise(inbox, norm_gain)

    after_low = shift(low, -1)
    before_high = shift(high, 1)
    before_low = shift(low, 1)
    after_high = shift(high, -1)
    across_low = shift(after_low, -1)
    across_high = shift(before_high, 1)

    projected = swap(projected_c, "z").reshape(Z, rows, Y, HEAD_SIZE)
    projected = projected.transpose(1, 2, 0, 3).reshape(rows, D)
    residual = hidden.astype(F32) + projected.astype(F32)
    attended = residual.astype(BF16)

    weights = (w_gate[0], w_up[0], w_down[0])
    own_low, own_high = expert(low, high, *weights)
    out_after_low, out_before_high = expert(after_low, before_high, *weights)
    out_before_low, out_after_high = expert(before_low, after_high, *weights)
    home_low = shift(out_before_low, -1)
    home_high = shift(out_after_high, 1)
    out_across_low, out_across_high = expert(across_low, across_high, *weights)
    far_low = shift(out_across_low, 1)
    far_high = shift(out_across_high, -1)
    sum_low = shift((out_after_low.astype(F32) + far_low.astype(F32)).astype(BF16), 1)
    sum_high = shift((out_before_high.astype(F32) + far_high.astype(F32)).astype(BF16), -1)
    home_low = own_low.astype(F32) + home_low.astype(F32) + sum_low.astype(F32)
    home_high = own_high.astype(F32) + home_high.astype(F32) + sum_high.astype(F32)
    returned = jnp.concatenate([home_low.astype(BF16), home_high.astype(BF16)], axis=0)

    back = swap(returned.reshape(LANES, Z * MOST, D), EXP).reshape(slots, D)
    gate = jnp.sum(jnp.where(named, gates_c[..., None], 0.0), axis=2)
    place = jnp.where(chosen, gate[..., None], 0.0).reshape(Z, rows, Z, LANES, MOST)
    place = lax.dynamic_index_in_dim(place, lax.axis_index("z"), 2, keepdims=False)
    place = jnp.where(same[:, None, None, :, None], place[:, :, :, None, :], 0.0)
    place = place.reshape(Z * rows, slots)
    place_high = place.astype(BF16)
    place_low = (place - place_high.astype(F32)).astype(BF16)
    moe_z = jnp.dot(place_high, back, preferred_element_type=F32) + jnp.dot(
        place_low, back, preferred_element_type=F32
    )
    moe = jnp.sum(swap(moe_z.astype(BF16).reshape(Z, rows, D), "z").astype(F32), axis=0)
    mixed = (residual + moe).astype(BF16)
    return (attended, mixed)


def solution(mesh):
    fine = Mesh(mesh.devices.reshape(Y, Z, X, CORE), CTX + EXP)
    every = CTX + EXP
    return jax.shard_map(
        on_device,
        mesh=fine,
        in_specs=(
            P(every, None),
            P(CTX, EXP),
            P(CTX, None),
            P(CTX, None),
            P(EXP, CTX),
            P(),
            P(every, None, None),
            P(every, None, None),
            P(every, None, None),
            P(every, None),
            P(every, None),
        ),
        out_specs=(P(every, None), P(every, None)),
        check_vma=False,
    )
```

```python
import jax
import jax.numpy as jnp
from jax import lax
from jax.experimental import pallas as pl
from jax.experimental.pallas import tpu as pltpu
from jax.sharding import Mesh
from jax.sharding import PartitionSpec as P

D = 4096
HEAD_SIZE = 128
QUERY_HEADS = 32
KEY_VALUE_HEADS = 2
TOPK = 8
MOST = 2
Y, Z, X, CORE = 4, 8, 4, 2
CTX = ("y", "z")
EXP = ("x", "core")
LANES = X * CORE
VMEM_LIMIT = 65024 * 1024
BF16 = jnp.bfloat16
F32 = jnp.float32


def spread(block, axes, count):
    return lax.all_to_all(
        jnp.broadcast_to(block[None], (count,) + block.shape), axes, 0, 0, tiled=True
    )


def swap(blocks, axes):
    return lax.all_to_all(blocks, axes, 0, 0, tiled=True)


def shift(block, step):
    return lax.ppermute(block, "y", [(i, (i + step) % Y) for i in range(Y)])


def norm_kernel(x_ref, gain_ref, low_ref, high_ref):
    lanes = LANES // 2
    rows, piece = lanes * x_ref.shape[1], x_ref.shape[2]
    for part, out_ref in enumerate((low_ref, high_ref)):

        def piece_of(i):
            x = x_ref[i * LANES + part * lanes : i * LANES + (part + 1) * lanes]
            return x.reshape(rows, piece).astype(F32)

        square = jnp.zeros((rows, 1), F32)
        for i in range(Z):
            x = piece_of(i)
            square = square + jnp.sum(x * x, axis=-1, keepdims=True)
        factor = lax.rsqrt(square * (1.0 / D) + 1e-06)
        for i in range(Z):
            x = piece_of(i) * factor
            for j in range(Y):
                at = (j * Z + i) * HEAD_SIZE
                out_ref[:, at : at + HEAD_SIZE] = (
                    x[:, j * HEAD_SIZE : (j + 1) * HEAD_SIZE] * gain_ref[:, at : at + HEAD_SIZE]
                ).astype(BF16)


def normalise(inbox, gain):
    rows = inbox.shape[0] * inbox.shape[1] // Z // 2
    return pl.pallas_call(
        norm_kernel,
        out_shape=[jax.ShapeDtypeStruct((rows, D), BF16)] * 2,
        in_specs=[pl.BlockSpec(memory_space=pltpu.VMEM)] * 2,
        out_specs=[pl.BlockSpec(memory_space=pltpu.VMEM)] * 2,
        compiler_params=pltpu.CompilerParams(vmem_limit_bytes=VMEM_LIMIT),
        cost_estimate=pl.CostEstimate(flops=6 * rows * D, bytes_accessed=8 * rows * D, transcendentals=0),
    )(inbox, gain.reshape(1, D))


STEPS = 4


def expert_kernel(low_ref, high_ref, gate_ref, up_ref, down_ref, *refs):
    out_low_ref, out_high_ref, gate_sum, up_sum, inner = refs[-5:]
    step = pl.program_id(0)
    depth = gate_ref.shape[0]
    rows = low_ref.shape[0]

    @pl.when(step < STEPS)
    def _():
        columns = pl.ds(pl.multiple_of(step * depth, depth), depth)
        x = jnp.concatenate([low_ref[:, columns], high_ref[:, columns]], axis=0)
        gate_h = jnp.dot(x, gate_ref[...], preferred_element_type=F32)
        up_h = jnp.dot(x, up_ref[...], preferred_element_type=F32)

        @pl.when(step == 0)
        def _():
            gate_sum[...] = gate_h
            up_sum[...] = up_h

        @pl.when(step > 0)
        def _():
            gate_sum[...] += gate_h
            up_sum[...] += up_h

    @pl.when(step == STEPS - 1)
    def _():
        v = gate_sum[...]
        inner[...] = (v / (1.0 + jnp.exp(-v)) * up_sum[...]).astype(BF16)

    @pl.when(step >= STEPS)
    def _():
        out = jnp.dot(inner[...], down_ref[...], preferred_element_type=F32).astype(BF16)
        out_low_ref[...] = out[:rows]
        out_high_ref[...] = out[rows:]


def expert(low, high, w_gate, w_up, w_down, after=()):
    rows = low.shape[0]
    width = w_gate.shape[1]
    piece = D // STEPS
    whole = pl.BlockSpec((rows, D), lambda i: (0, 0))
    into = pl.BlockSpec((piece, width), lambda i: (jnp.minimum(i, STEPS - 1), 0))
    out_of = pl.BlockSpec((width, piece), lambda i: (0, jnp.maximum(i - STEPS, 0)))
    result = pl.BlockSpec((rows, piece), lambda i: (0, jnp.maximum(i - STEPS, 0)))
    return pl.pallas_call(
        expert_kernel,
        grid=(2 * STEPS,),
        out_shape=[jax.ShapeDtypeStruct((rows, D), BF16)] * 2,
        in_specs=[whole, whole, into, into, out_of]
        + [pl.BlockSpec((rows // 4, HEAD_SIZE), lambda i: (0, 0)) for _ in after],
        out_specs=[result, result],
        scratch_shapes=[
            pltpu.VMEM((2 * rows, width), F32),
            pltpu.VMEM((2 * rows, width), F32),
            pltpu.VMEM((2 * rows, width), BF16),
        ],
        compiler_params=pltpu.CompilerParams(
            dimension_semantics=("arbitrary",), vmem_limit_bytes=VMEM_LIMIT
        ),
        cost_estimate=pl.CostEstimate(
            flops=12 * rows * D * width,
            bytes_accessed=6 * D * width + 8 * rows * D,
            transcendentals=2 * rows * width,
        ),
    )(low, high, w_gate, w_up, w_down, *after)


def slots_of(routes):
    experts = jnp.arange(Z * LANES, dtype=jnp.int32)
    named = routes[..., None] == experts
    hit = jnp.any(named, axis=-2)
    count = hit.astype(jnp.int32)
    earlier = jnp.cumsum(count, axis=-2) - count
    chosen = hit[..., None] & (earlier[..., None] == jnp.arange(MOST, dtype=jnp.int32))
    return chosen, named


def on_device(
    hidden, queries, keys, values, out_weight, norm_gain, w_gate, w_up, w_down, routes, gates
):
    rows_ctx = queries.shape[0]
    heads = queries.shape[1] // HEAD_SIZE
    rows = routes.shape[0]
    piece = D // Z
    lane = lax.axis_index(EXP)
    ctx = lax.axis_index(CTX)
    core = lax.axis_index("core")
    scale = HEAD_SIZE ** (-0.5)

    pieces = [out_weight] + [shift(out_weight, step) for step in range(1, Y)]
    by_distance = jnp.stack(pieces[::-1] * 2)
    weight_y = lax.dynamic_slice_in_dim(by_distance, Y - 1 - lax.axis_index("y"), Y, 0)
    weight_y = weight_y.transpose(1, 0, 2).reshape(out_weight.shape[0], piece)

    group = lax.axis_index("z")
    hidden_z = hidden.reshape(rows, Y, Z, HEAD_SIZE).transpose(2, 0, 1, 3).reshape(Z, rows, piece)
    gates_high = gates.astype(BF16)
    gates_rest = gates - gates_high.astype(F32)
    gates_mid = gates_rest.astype(BF16)
    gates_low = (gates_rest - gates_mid.astype(F32)).astype(BF16)
    table = jnp.concatenate([routes.astype(BF16), gates_high, gates_mid, gates_low], axis=1)
    table = jnp.pad(table, ((0, 0), (0, HEAD_SIZE - table.shape[1])))
    parcels = jnp.concatenate(
        [hidden_z, jnp.broadcast_to(table[None], (Z, rows, HEAD_SIZE))], axis=2
    )
    parcels = jnp.concatenate([parcels, parcels], axis=0)
    parcels = lax.dynamic_slice_in_dim(parcels, group, Z, 0)
    pieces = [parcels[0]] + [
        lax.ppermute(parcels[step], "z", [(i, (i + step) % Z) for i in range(Z)])
        for step in range(1, Z)
    ]
    by_distance = jnp.stack(pieces[::-1] * 2)
    parcels = lax.dynamic_slice_in_dim(by_distance, Z - 1 - group, Z, 0)
    hidden_c = parcels[:, :, :piece].astype(F32)
    table_c = parcels[:, :, piece : piece + 4 * TOPK].astype(F32).reshape(Z, rows, 4, TOPK)
    routes_c = table_c[:, :, 0].astype(jnp.int32)
    gates_c = table_c[:, :, 1] + table_c[:, :, 2] + table_c[:, :, 3]

    head = lane * heads // (QUERY_HEADS // KEY_VALUE_HEADS)
    half_ctx = rows_ctx // CORE
    key_head = lax.dynamic_slice(keys, (core * half_ctx, head * HEAD_SIZE), (half_ctx, HEAD_SIZE))
    value_head = lax.dynamic_slice(
        values, (core * half_ctx, head * HEAD_SIZE), (half_ctx, HEAD_SIZE)
    )
    mine = spread(jnp.concatenate([key_head, value_head], axis=1), CTX, Y * Z)
    mine = mine.reshape(Y * Z * half_ctx, 2 * HEAD_SIZE)
    other = lax.ppermute(mine, "core", [(0, 1), (1, 0)])
    query_rows = queries.reshape(rows_ctx * heads, HEAD_SIZE)
    query_pos = ctx * rows_ctx + jnp.arange(rows_ctx * heads, dtype=jnp.int32) // heads
    index = jnp.arange(Y * Z * half_ctx, dtype=jnp.int32)
    base_pos = (index // half_ctx) * rows_ctx + index % half_ctx
    scored = []
    for both, part in ((mine, core), (other, 1 - core)):
        scores = (
            jnp.einsum(
                "qd,kd->qk", query_rows, both[:, :HEAD_SIZE], preferred_element_type=F32
            )
            * scale
        )
        visible = (base_pos + part * half_ctx)[None, :] <= query_pos[:, None]
        scored.append((jnp.where(visible, scores, -1e30), visible, both[:, HEAD_SIZE:]))
    peak = jnp.maximum(jnp.max(scored[0][0], axis=-1), jnp.max(scored[1][0], axis=-1))
    totals, accumulated = 0.0, 0.0
    for scores, visible, value_piece in scored:
        weights = jnp.where(visible, jnp.exp(scores - peak[:, None]), 0.0)
        totals = totals + jnp.sum(weights, axis=-1)
        accumulated = accumulated + jnp.dot(
            weights.astype(BF16), value_piece, preferred_element_type=F32
        )
    attention = (
        (accumulated / totals[:, None]).reshape(rows_ctx, heads * HEAD_SIZE).astype(BF16)
    )

    attention_z = spread(attention, "z", Z).reshape(Z, LANES, rows, piece)

    partial = jnp.einsum("zerf,fc->ezrc", attention_z, weight_y, preferred_element_type=F32)
    projected_c = jnp.sum(swap(partial.astype(BF16), EXP).astype(F32), axis=0)
    residual_c = (hidden_c + projected_c).astype(BF16).reshape(Z * rows, piece)

    chosen, named = slots_of(routes_c)
    same = jnp.eye(Z, dtype=bool)
    pick = chosen.transpose(2, 0, 3, 1)[:, :, :, None, :] & same[None, :, None, :, None]
    pick = pick.reshape(Z * LANES * Z * MOST, Z * rows).astype(BF16)
    outbox = jnp.dot(pick, residual_c, preferred_element_type=F32).astype(BF16)
    inbox = swap(outbox.reshape(Z * LANES, Z * MOST, piece), ("z",) + EXP)
    inbox, projected_c = lax.optimization_barrier((inbox, projected_c.astype(BF16)))
    slots = LANES * Z * MOST
    low, high = normalise(inbox, norm_gain)

    after_low = shift(low, -1)
    before_high = shift(high, 1)
    before_low = shift(low, 1)
    after_high = shift(high, -1)
    across_low = shift(after_low, -1)
    across_high = shift(before_high, 1)

    projected = swap(projected_c, "z").reshape(Z, rows, Y, HEAD_SIZE)
    projected = projected.transpose(1, 2, 0, 3).reshape(rows, D)
    residual = hidden.astype(F32) + projected.astype(F32)
    attended = residual.astype(BF16)

    weights = (w_gate[0], w_up[0], w_down[0])
    own_low, own_high = expert(low, high, *weights)
    out_after_low, out_before_high = expert(
        after_low, before_high, *weights, after=(own_low, jnp.tile(projected, (2, 1)))
    )
    out_across_low, out_across_high = expert(
        across_low, across_high, *weights, after=(out_after_low,)
    )
    out_before_low, out_after_high = expert(
        before_low, after_high, *weights, after=(out_across_low,)
    )
    home_low = shift(out_before_low, -1)
    home_high = shift(out_after_high, 1)
    far_low = shift(out_across_low, 1)
    far_high = shift(out_across_high, -1)
    sum_low = shift((out_after_low.astype(F32) + far_low.astype(F32)).astype(BF16), 1)
    sum_high = shift((out_before_high.astype(F32) + far_high.astype(F32)).astype(BF16), -1)
    home_low = own_low.astype(F32) + home_low.astype(F32) + sum_low.astype(F32)
    home_high = own_high.astype(F32) + home_high.astype(F32) + sum_high.astype(F32)
    returned = jnp.concatenate([home_low.astype(BF16), home_high.astype(BF16)], axis=0)

    back = swap(returned.reshape(LANES, Z * MOST, D), EXP).reshape(slots, D)
    gate = jnp.sum(jnp.where(named, gates_c[..., None], 0.0), axis=2)
    place = jnp.where(chosen, gate[..., None], 0.0).reshape(Z, rows, Z, LANES, MOST)
    place = lax.dynamic_index_in_dim(place, lax.axis_index("z"), 2, keepdims=False)
    place = jnp.where(same[:, None, None, :, None], place[:, :, :, None, :], 0.0)
    place = place.reshape(Z * rows, slots)
    place_high = place.astype(BF16)
    place_low = (place - place_high.astype(F32)).astype(BF16)
    moe_z = jnp.dot(place_high, back, preferred_element_type=F32) + jnp.dot(
        place_low, back, preferred_element_type=F32
    )
    moe = jnp.sum(swap(moe_z.astype(BF16).reshape(Z, rows, D), "z").astype(F32), axis=0)
    mixed = (residual + moe).astype(BF16)
    return (attended, mixed)


def solution(mesh):
    fine = Mesh(mesh.devices.reshape(Y, Z, X, CORE), CTX + EXP)
    every = CTX + EXP
    return jax.shard_map(
        on_device,
        mesh=fine,
        in_specs=(
            P(every, None),
            P(CTX, EXP),
            P(CTX, None),
            P(CTX, None),
            P(EXP, CTX),
            P(),
            P(every, None, None),
            P(every, None, None),
            P(every, None, None),
            P(every, None),
            P(every, None),
        ),
        out_specs=(P(every, None), P(every, None)),
        check_vma=False,
    )
```

```python
import functools

import jax
import jax.numpy as jnp
from jax import lax
from jax.experimental import pallas as pl
from jax.experimental.pallas import tpu as pltpu
from jax.sharding import Mesh
from jax.sharding import PartitionSpec as P

D = 4096
HEAD_SIZE = 128
QUERY_HEADS = 32
KEY_VALUE_HEADS = 2
TOPK = 8
MOST = 2
Y, Z, X, CORE = 4, 8, 4, 2
CTX = ("y", "z")
EXP = ("x", "core")
LANES = X * CORE
VMEM_LIMIT = 65024 * 1024
BF16 = jnp.bfloat16
F32 = jnp.float32


def spread(block, axes, count):
    return lax.all_to_all(
        jnp.broadcast_to(block[None], (count,) + block.shape), axes, 0, 0, tiled=True
    )


def swap(blocks, axes):
    return lax.all_to_all(blocks, axes, 0, 0, tiled=True)


def shift(block, step):
    return lax.ppermute(block, "y", [(i, (i + step) % Y) for i in range(Y)])


def norm_kernel(x_ref, gain_ref, low_ref, high_ref):
    lanes = LANES // 2
    rows, piece = lanes * x_ref.shape[1], x_ref.shape[2]
    for part, out_ref in enumerate((low_ref, high_ref)):

        def piece_of(i):
            x = x_ref[i * LANES + part * lanes : i * LANES + (part + 1) * lanes]
            return x.reshape(rows, piece).astype(F32)

        square = jnp.zeros((rows, 1), F32)
        for i in range(Z):
            x = piece_of(i)
            square = square + jnp.sum(x * x, axis=-1, keepdims=True)
        factor = lax.rsqrt(square * (1.0 / D) + 1e-06)
        for i in range(Z):
            x = piece_of(i) * factor
            for j in range(Y):
                at = (j * Z + i) * HEAD_SIZE
                out_ref[:, at : at + HEAD_SIZE] = (
                    x[:, j * HEAD_SIZE : (j + 1) * HEAD_SIZE] * gain_ref[:, at : at + HEAD_SIZE]
                ).astype(BF16)


def normalise(inbox, gain):
    rows = inbox.shape[0] * inbox.shape[1] // Z // 2
    return pl.pallas_call(
        norm_kernel,
        out_shape=[jax.ShapeDtypeStruct((rows, D), BF16)] * 2,
        in_specs=[pl.BlockSpec(memory_space=pltpu.VMEM)] * 2,
        out_specs=[pl.BlockSpec(memory_space=pltpu.VMEM)] * 2,
        compiler_params=pltpu.CompilerParams(vmem_limit_bytes=VMEM_LIMIT),
        cost_estimate=pl.CostEstimate(flops=6 * rows * D, bytes_accessed=8 * rows * D, transcendentals=0),
    )(inbox, gain.reshape(1, D))


STEPS = 4


def expert_kernel(count, *refs):
    blocks, (gate_ref, up_ref, down_ref) = refs[:count], refs[count : count + 3]
    x, gate_w, up_w, down_w, out, in_sems, weight_sems, out_sems = refs[-8:]
    outs = refs[-8 - count : -8]
    rows = blocks[0].shape[0]
    piece = D // STEPS
    parts = [slice(i * piece, (i + 1) * piece) for i in range(STEPS)]
    own_rows = [slice(j * rows, (j + 1) * rows) for j in range(count)]
    row_copies, weight_copies, down_copies, out_copies = [], [], [], []
    for i, part in enumerate(parts):
        row_copies.append(
            [
                pltpu.make_async_copy(block.at[:, part], x.at[own, part], in_sems.at[i, j])
                for j, (block, own) in enumerate(zip(blocks, own_rows))
            ]
        )
        weight_copies.append(
            [
                pltpu.make_async_copy(gate_ref.at[part], gate_w.at[part], weight_sems.at[0, i]),
                pltpu.make_async_copy(up_ref.at[part], up_w.at[part], weight_sems.at[1, i]),
            ]
        )
        down_copies.append(
            pltpu.make_async_copy(down_ref.at[:, part], down_w.at[:, part], weight_sems.at[2, i])
        )
        out_copies.append(
            [
                pltpu.make_async_copy(out.at[own, part], out_ref.at[:, part], out_sems.at[i, j])
                for j, (out_ref, own) in enumerate(zip(outs, own_rows))
            ]
        )
    for i in range(STEPS):
        for copy in row_copies[i] + weight_copies[i]:
            copy.start()
    for copy in down_copies:
        copy.start()
    gate_h, up_h = 0.0, 0.0
    for i, part in enumerate(parts):
        for copy in row_copies[i] + weight_copies[i]:
            copy.wait()
        gate_h = gate_h + jnp.dot(x[:, part], gate_w[part], preferred_element_type=F32)
        up_h = up_h + jnp.dot(x[:, part], up_w[part], preferred_element_type=F32)
    inner = (gate_h / (1.0 + jnp.exp(-gate_h)) * up_h).astype(BF16)
    for i, part in enumerate(parts):
        down_copies[i].wait()
        out[:, part] = jnp.dot(inner, down_w[:, part], preferred_element_type=F32).astype(BF16)
        for copy in out_copies[i]:
            copy.start()
    for copies in out_copies:
        for copy in copies:
            copy.wait()


def expert(blocks, weights, after=()):
    rows = blocks[0].shape[0]
    count = len(blocks)
    width = weights[0].shape[1]
    return pl.pallas_call(
        functools.partial(expert_kernel, count),
        out_shape=[jax.ShapeDtypeStruct((rows, D), BF16)] * count,
        in_specs=[pl.BlockSpec(memory_space=pl.ANY)] * (count + 3 + len(after)),
        out_specs=[pl.BlockSpec(memory_space=pl.ANY)] * count,
        scratch_shapes=[
            pltpu.VMEM((count * rows, D), BF16),
            pltpu.VMEM((D, width), BF16),
            pltpu.VMEM((D, width), BF16),
            pltpu.VMEM((width, D), BF16),
            pltpu.VMEM((count * rows, D), BF16),
            pltpu.SemaphoreType.DMA((STEPS, count)),
            pltpu.SemaphoreType.DMA((3, STEPS)),
            pltpu.SemaphoreType.DMA((STEPS, count)),
        ],
        compiler_params=pltpu.CompilerParams(vmem_limit_bytes=VMEM_LIMIT),
        cost_estimate=pl.CostEstimate(
            flops=6 * count * rows * D * width,
            bytes_accessed=6 * D * width + 4 * count * rows * D,
            transcendentals=count * rows * width,
        ),
    )(*blocks, *weights, *after)


def add_kernel(count, *refs):
    out_ref = refs[-1]
    rows = refs[0].shape[0]
    for i in range(2):
        total = refs[i * count][...].astype(F32)
        for ref in refs[i * count + 1 : (i + 1) * count]:
            total = total + ref[...].astype(F32)
        out_ref[i * rows : (i + 1) * rows] = total.astype(BF16)


def pair_kernel(count, *refs):
    for i, out_ref in enumerate(refs[-2:]):
        total = refs[i * count][...].astype(F32)
        for ref in refs[i * count + 1 : (i + 1) * count]:
            total = total + ref[...].astype(F32)
        out_ref[...] = total.astype(BF16)


def add_up(terms, after, joined):
    rows = terms[0][0].shape[0]
    count = len(terms[0])
    piece = D // 2
    block = pl.BlockSpec((rows, piece), lambda i: (0, i))
    if joined:
        kernel, blocks, results = add_kernel, pl.BlockSpec((2 * rows, piece), lambda i: (0, i)), 1
    else:
        kernel, blocks, results = pair_kernel, block, 2
    return pl.pallas_call(
        functools.partial(kernel, count),
        grid=(D // piece,),
        out_shape=[jax.ShapeDtypeStruct((2 * rows // results, D), BF16)] * results,
        in_specs=[block] * (2 * count) + [pl.BlockSpec(memory_space=pl.ANY) for _ in after],
        out_specs=[blocks] * results,
        compiler_params=pltpu.CompilerParams(
            dimension_semantics=("arbitrary",), vmem_limit_bytes=VMEM_LIMIT
        ),
        cost_estimate=pl.CostEstimate(
            flops=2 * count * rows * D,
            bytes_accessed=4 * (count + 1) * rows * D,
            transcendentals=0,
        ),
    )(*terms[0], *terms[1], *after)


def slots_of(routes):
    experts = jnp.arange(Z * LANES, dtype=jnp.int32)
    named = routes[..., None] == experts
    hit = jnp.any(named, axis=-2)
    count = hit.astype(jnp.int32)
    earlier = jnp.cumsum(count, axis=-2) - count
    chosen = hit[..., None] & (earlier[..., None] == jnp.arange(MOST, dtype=jnp.int32))
    return chosen, named


def on_device(
    hidden, queries, keys, values, out_weight, norm_gain, w_gate, w_up, w_down, routes, gates
):
    rows_ctx = queries.shape[0]
    heads = queries.shape[1] // HEAD_SIZE
    rows = routes.shape[0]
    piece = D // Z
    lane = lax.axis_index(EXP)
    ctx = lax.axis_index(CTX)
    core = lax.axis_index("core")
    scale = HEAD_SIZE ** (-0.5)

    pieces = [out_weight] + [shift(out_weight, step) for step in range(1, Y)]
    by_distance = jnp.stack(pieces[::-1] * 2)
    weight_y = lax.dynamic_slice_in_dim(by_distance, Y - 1 - lax.axis_index("y"), Y, 0)
    weight_y = weight_y.transpose(1, 0, 2).reshape(out_weight.shape[0], piece)

    head = lane * heads // (QUERY_HEADS // KEY_VALUE_HEADS)
    half_ctx = rows_ctx // CORE
    key_head = lax.dynamic_slice(keys, (core * half_ctx, head * HEAD_SIZE), (half_ctx, HEAD_SIZE))
    value_head = lax.dynamic_slice(
        values, (core * half_ctx, head * HEAD_SIZE), (half_ctx, HEAD_SIZE)
    )
    mine = spread(jnp.concatenate([key_head, value_head], axis=1), CTX, Y * Z)
    mine = mine.reshape(Y * Z * half_ctx, 2 * HEAD_SIZE)
    other = lax.ppermute(mine, "core", [(0, 1), (1, 0)])
    query_rows = queries.reshape(rows_ctx * heads, HEAD_SIZE)
    query_pos = ctx * rows_ctx + jnp.arange(rows_ctx * heads, dtype=jnp.int32) // heads
    index = jnp.arange(Y * Z * half_ctx, dtype=jnp.int32)
    base_pos = (index // half_ctx) * rows_ctx + index % half_ctx
    scored = []
    for both, part in ((mine, core), (other, 1 - core)):
        scores = (
            jnp.einsum(
                "qd,kd->qk", query_rows, both[:, :HEAD_SIZE], preferred_element_type=F32
            )
            * scale
        )
        visible = (base_pos + part * half_ctx)[None, :] <= query_pos[:, None]
        scored.append((jnp.where(visible, scores, -1e30), visible, both[:, HEAD_SIZE:]))
    peak = jnp.maximum(jnp.max(scored[0][0], axis=-1), jnp.max(scored[1][0], axis=-1))
    totals, accumulated = 0.0, 0.0
    for scores, visible, value_piece in scored:
        weights = jnp.where(visible, jnp.exp(scores - peak[:, None]), 0.0)
        totals = totals + jnp.sum(weights, axis=-1)
        accumulated = accumulated + jnp.dot(
            weights.astype(BF16), value_piece, preferred_element_type=F32
        )
    attention = (
        (accumulated / totals[:, None]).reshape(rows_ctx, heads * HEAD_SIZE).astype(BF16)
    )

    hidden_z = hidden.reshape(rows, Y, Z, HEAD_SIZE).transpose(2, 0, 1, 3).reshape(Z, rows, piece)
    gates_high = gates.astype(BF16)
    gates_rest = gates - gates_high.astype(F32)
    gates_mid = gates_rest.astype(BF16)
    gates_low = (gates_rest - gates_mid.astype(F32)).astype(BF16)
    table = jnp.concatenate([routes.astype(BF16), gates_high, gates_mid, gates_low], axis=1)
    table = jnp.pad(table, ((0, 0), (0, piece - table.shape[1])))
    parcel = jnp.concatenate(
        [
            jnp.broadcast_to(attention[None], (Z, rows_ctx, piece)),
            hidden_z,
            jnp.broadcast_to(table[None], (Z, rows, piece)),
        ],
        axis=1,
    )
    parcel = swap(parcel, "z")
    attention_z = parcel[:, :rows_ctx].reshape(Z, LANES, rows, piece)
    hidden_c = parcel[:, rows_ctx : rows_ctx + rows].astype(F32)
    table_c = parcel[:, rows_ctx + rows :, : 4 * TOPK].astype(F32).reshape(Z, rows, 4, TOPK)
    routes_c = table_c[:, :, 0].astype(jnp.int32)
    gates_c = table_c[:, :, 1] + table_c[:, :, 2] + table_c[:, :, 3]

    partial = jnp.einsum("zerf,fc->ezrc", attention_z, weight_y, preferred_element_type=F32)
    projected_c = jnp.sum(swap(partial.astype(BF16), EXP).astype(F32), axis=0)
    residual_c = (hidden_c + projected_c).astype(BF16).reshape(Z * rows, piece)

    chosen, named = slots_of(routes_c)
    same = jnp.eye(Z, dtype=bool)
    pick = chosen.transpose(2, 0, 3, 1)[:, :, :, None, :] & same[None, :, None, :, None]
    pick = pick.reshape(Z * LANES * Z * MOST, Z * rows).astype(BF16)
    outbox = jnp.dot(pick, residual_c, preferred_element_type=F32).astype(BF16)
    inbox = swap(outbox.reshape(Z * LANES, Z * MOST, piece), ("z",) + EXP)
    slots = LANES * Z * MOST
    low, high = normalise(inbox, norm_gain)

    after_low = shift(low, -1)
    before_high = shift(high, 1)
    before_low = shift(low, 1)
    after_high = shift(high, -1)
    across_low = shift(after_low, -1)
    across_high = shift(before_high, 1)

    projected = swap(projected_c.astype(BF16), "z").reshape(Z, rows, Y, HEAD_SIZE)
    projected = projected.transpose(1, 2, 0, 3).reshape(rows, D)

    weights = (w_gate[0], w_up[0], w_down[0])
    (
        own_low,
        own_high,
        out_after_low,
        out_before_high,
        out_before_low,
        out_after_high,
    ) = expert(
        (low, high, after_low, before_high, before_low, after_high), weights, after=(projected,)
    )
    out_across_low, out_across_high = expert(
        (across_low, across_high), weights, after=(own_low,)
    )
    home_low = shift(out_before_low, -1)
    home_high = shift(out_after_high, 1)
    far_low = shift(out_across_low, 1)
    far_high = shift(out_across_high, -1)
    sum_low, sum_high = add_up(
        ((out_after_low, far_low), (out_before_high, far_high)), (home_low, home_high), False
    )
    sum_low, sum_high = shift(sum_low, 1), shift(sum_high, -1)
    (returned,) = add_up(
        ((own_low, home_low, sum_low), (own_high, home_high, sum_high)), (), True
    )

    back = swap(returned.reshape(LANES, Z * MOST, D), EXP).reshape(slots, D)
    gate = jnp.sum(jnp.where(named, gates_c[..., None], 0.0), axis=2)
    place = jnp.where(chosen, gate[..., None], 0.0).reshape(Z, rows, Z, LANES, MOST)
    place = lax.dynamic_index_in_dim(place, lax.axis_index("z"), 2, keepdims=False)
    place = jnp.where(same[:, None, None, :, None], place[:, :, :, None, :], 0.0)
    place = place.reshape(Z * rows, slots)
    place_high = place.astype(BF16)
    place_low = (place - place_high.astype(F32)).astype(BF16)
    moe_z = jnp.dot(place_high, back, preferred_element_type=F32) + jnp.dot(
        place_low, back, preferred_element_type=F32
    )
    moe = jnp.sum(swap(moe_z.astype(BF16).reshape(Z, rows, D), "z").astype(F32), axis=0)
    residual = hidden.astype(F32) + projected.astype(F32)
    attended = residual.astype(BF16)
    mixed = (residual + moe).astype(BF16)
    return (attended, mixed)


def solution(mesh):
    fine = Mesh(mesh.devices.reshape(Y, Z, X, CORE), CTX + EXP)
    every = CTX + EXP
    return jax.shard_map(
        on_device,
        mesh=fine,
        in_specs=(
            P(every, None),
            P(CTX, EXP),
            P(CTX, None),
            P(CTX, None),
            P(EXP, CTX),
            P(),
            P(every, None, None),
            P(every, None, None),
            P(every, None, None),
            P(every, None),
            P(every, None),
        ),
        out_specs=(P(every, None), P(every, None)),
        check_vma=False,
    )
```

```python
import functools

import jax
import jax.numpy as jnp
from jax import lax
from jax.experimental import pallas as pl
from jax.experimental.pallas import tpu as pltpu
from jax.sharding import Mesh
from jax.sharding import PartitionSpec as P

D = 4096
HEAD_SIZE = 128
QUERY_HEADS = 32
KEY_VALUE_HEADS = 2
TOPK = 8
MOST = 2
Y, Z, X, CORE = 4, 8, 4, 2
CTX = ("y", "z")
EXP = ("x", "core")
LANES = X * CORE
VMEM_LIMIT = 20 * 1024 * 1024
BF16 = jnp.bfloat16
F32 = jnp.float32


def spread(block, axes, count):
    return lax.all_to_all(
        jnp.broadcast_to(block[None], (count,) + block.shape), axes, 0, 0, tiled=True
    )


def swap(blocks, axes):
    return lax.all_to_all(blocks, axes, 0, 0, tiled=True)


def shift(block, step):
    return lax.ppermute(block, "y", [(i, (i + step) % Y) for i in range(Y)])


def norm_kernel(x_ref, gain_ref, low_ref, high_ref):
    lanes = LANES // 2
    rows, piece = lanes * x_ref.shape[1], x_ref.shape[2]
    for part, out_ref in enumerate((low_ref, high_ref)):

        def piece_of(i):
            x = x_ref[i * LANES + part * lanes : i * LANES + (part + 1) * lanes]
            return x.reshape(rows, piece).astype(F32)

        square = jnp.zeros((rows, 1), F32)
        for i in range(Z):
            x = piece_of(i)
            square = square + jnp.sum(x * x, axis=-1, keepdims=True)
        factor = lax.rsqrt(square * (1.0 / D) + 1e-06)
        for i in range(Z):
            x = piece_of(i) * factor
            for j in range(Y):
                at = (j * Z + i) * HEAD_SIZE
                out_ref[:, at : at + HEAD_SIZE] = (
                    x[:, j * HEAD_SIZE : (j + 1) * HEAD_SIZE] * gain_ref[:, at : at + HEAD_SIZE]
                ).astype(BF16)


def normalise(inbox, gain):
    rows = inbox.shape[0] * inbox.shape[1] // Z // 2
    return pl.pallas_call(
        norm_kernel,
        out_shape=[jax.ShapeDtypeStruct((rows, D), BF16)] * 2,
        in_specs=[pl.BlockSpec(memory_space=pltpu.VMEM)] * 2,
        out_specs=[pl.BlockSpec(memory_space=pltpu.VMEM)] * 2,
        compiler_params=pltpu.CompilerParams(vmem_limit_bytes=VMEM_LIMIT),
        cost_estimate=pl.CostEstimate(flops=6 * rows * D, bytes_accessed=8 * rows * D, transcendentals=0),
    )(inbox, gain.reshape(1, D))


STEPS = 4


def load_kernel(*refs):
    sources, targets, sems = refs[:3], refs[-4:-1], refs[-1]
    copies = [
        pltpu.make_async_copy(source, target, sems.at[i])
        for i, (source, target) in enumerate(zip(sources, targets))
    ]
    for copy in copies:
        copy.start()
    for copy in copies:
        copy.wait()


def load(arrays, after):
    return pl.pallas_call(
        load_kernel,
        out_shape=[pltpu.VMEM(array.shape, array.dtype) for array in arrays],
        in_specs=[pl.BlockSpec(memory_space=pl.ANY)] * (len(arrays) + len(after)),
        out_specs=[pl.BlockSpec(memory_space=pltpu.VMEM)] * len(arrays),
        scratch_shapes=[pltpu.SemaphoreType.DMA((len(arrays),))],
        compiler_params=pltpu.CompilerParams(vmem_limit_bytes=16 * 1024 * 1024),
    )(*arrays, *after)


def expert_kernel(count, *refs):
    blocks, (gate_w, up_w, down_w) = refs[:count], refs[count : count + 3]
    x, out, in_sems, out_sems = refs[-4:]
    outs = refs[-4 - count : -4]
    rows = blocks[0].shape[0]
    piece = D // STEPS
    parts = [slice(i * piece, (i + 1) * piece) for i in range(STEPS)]
    own_rows = [slice(j * rows, (j + 1) * rows) for j in range(count)]
    row_copies, out_copies = [], []
    for i, part in enumerate(parts):
        row_copies.append(
            [
                pltpu.make_async_copy(block.at[:, part], x.at[own, part], in_sems.at[i, j])
                for j, (block, own) in enumerate(zip(blocks, own_rows))
            ]
        )
        out_copies.append(
            [
                pltpu.make_async_copy(out.at[own, part], out_ref.at[:, part], out_sems.at[i, j])
                for j, (out_ref, own) in enumerate(zip(outs, own_rows))
            ]
        )
    for copies in row_copies:
        for copy in copies:
            copy.start()
    gate_h, up_h = 0.0, 0.0
    for i, part in enumerate(parts):
        for copy in row_copies[i]:
            copy.wait()
        gate_h = gate_h + jnp.dot(x[:, part], gate_w[part], preferred_element_type=F32)
        up_h = up_h + jnp.dot(x[:, part], up_w[part], preferred_element_type=F32)
    inner = (gate_h / (1.0 + jnp.exp(-gate_h)) * up_h).astype(BF16)
    for i, part in enumerate(parts):
        out[:, part] = jnp.dot(inner, down_w[:, part], preferred_element_type=F32).astype(BF16)
        for copy in out_copies[i]:
            copy.start()
    for copies in out_copies:
        for copy in copies:
            copy.wait()


def expert(blocks, weights, after=()):
    rows = blocks[0].shape[0]
    count = len(blocks)
    width = weights[0].shape[1]
    return pl.pallas_call(
        functools.partial(expert_kernel, count),
        out_shape=[jax.ShapeDtypeStruct((rows, D), BF16)] * count,
        in_specs=[pl.BlockSpec(memory_space=pl.ANY)] * count
        + [pl.BlockSpec(memory_space=pltpu.VMEM)] * 3
        + [pl.BlockSpec(memory_space=pl.ANY)] * len(after),
        out_specs=[pl.BlockSpec(memory_space=pl.ANY)] * count,
        scratch_shapes=[
            pltpu.VMEM((count * rows, D), BF16),
            pltpu.VMEM((count * rows, D), BF16),
            pltpu.SemaphoreType.DMA((STEPS, count)),
            pltpu.SemaphoreType.DMA((STEPS, count)),
        ],
        compiler_params=pltpu.CompilerParams(vmem_limit_bytes=VMEM_LIMIT),
        cost_estimate=pl.CostEstimate(
            flops=6 * count * rows * D * width,
            bytes_accessed=6 * D * width + 4 * count * rows * D,
            transcendentals=count * rows * width,
        ),
    )(*blocks, *weights, *after)


def hand_on_kernel(*refs):
    pass


def hand_on(blocks, after):
    count = len(blocks)
    return pl.pallas_call(
        hand_on_kernel,
        out_shape=[jax.ShapeDtypeStruct(block.shape, block.dtype) for block in blocks],
        in_specs=[pl.BlockSpec(memory_space=pl.ANY)] * (count + len(after)),
        out_specs=[pl.BlockSpec(memory_space=pl.ANY)] * count,
        input_output_aliases={i: i for i in range(count)},
    )(*blocks, *after)


def pair_kernel(*refs):
    for i, out_ref in enumerate(refs[-2:]):
        out_ref[...] = (refs[2 * i][...].astype(F32) + refs[2 * i + 1][...].astype(F32)).astype(BF16)


def add_pairs(low, high, after):
    rows = low[0].shape[0]
    piece = D // 2
    block = pl.BlockSpec((rows, piece), lambda i: (0, i))
    return pl.pallas_call(
        pair_kernel,
        grid=(D // piece,),
        out_shape=[jax.ShapeDtypeStruct((rows, D), BF16)] * 2,
        in_specs=[block] * 4 + [pl.BlockSpec(memory_space=pl.ANY) for _ in after],
        out_specs=[block] * 2,
        compiler_params=pltpu.CompilerParams(
            dimension_semantics=("arbitrary",), vmem_limit_bytes=16 * 1024 * 1024
        ),
        cost_estimate=pl.CostEstimate(
            flops=2 * rows * D, bytes_accessed=12 * rows * D, transcendentals=0
        ),
    )(*low, *high, *after)


def slots_of(routes):
    experts = jnp.arange(Z * LANES, dtype=jnp.int32)
    named = routes[..., None] == experts
    hit = jnp.any(named, axis=-2)
    count = hit.astype(jnp.int32)
    earlier = jnp.cumsum(count, axis=-2) - count
    chosen = hit[..., None] & (earlier[..., None] == jnp.arange(MOST, dtype=jnp.int32))
    return chosen, named


def on_device(
    hidden, queries, keys, values, out_weight, norm_gain, w_gate, w_up, w_down, routes, gates
):
    rows_ctx = queries.shape[0]
    heads = queries.shape[1] // HEAD_SIZE
    rows = routes.shape[0]
    piece = D // Z
    lane = lax.axis_index(EXP)
    ctx = lax.axis_index(CTX)
    core = lax.axis_index("core")
    scale = HEAD_SIZE ** (-0.5)

    pieces = [out_weight] + [shift(out_weight, step) for step in range(1, Y)]
    by_distance = jnp.stack(pieces[::-1] * 2)
    weight_y = lax.dynamic_slice_in_dim(by_distance, Y - 1 - lax.axis_index("y"), Y, 0)
    weight_y = weight_y.transpose(1, 0, 2).reshape(out_weight.shape[0], piece)

    head = lane * heads // (QUERY_HEADS // KEY_VALUE_HEADS)
    half_ctx = rows_ctx // CORE
    key_head = lax.dynamic_slice(keys, (core * half_ctx, head * HEAD_SIZE), (half_ctx, HEAD_SIZE))
    value_head = lax.dynamic_slice(
        values, (core * half_ctx, head * HEAD_SIZE), (half_ctx, HEAD_SIZE)
    )
    mine = spread(jnp.concatenate([key_head, value_head], axis=1), CTX, Y * Z)
    mine = mine.reshape(Y * Z * half_ctx, 2 * HEAD_SIZE)
    other = lax.ppermute(mine, "core", [(0, 1), (1, 0)])
    query_rows = queries.reshape(rows_ctx * heads, HEAD_SIZE)
    query_pos = ctx * rows_ctx + jnp.arange(rows_ctx * heads, dtype=jnp.int32) // heads
    index = jnp.arange(Y * Z * half_ctx, dtype=jnp.int32)
    base_pos = (index // half_ctx) * rows_ctx + index % half_ctx
    scored = []
    for both, part in ((mine, core), (other, 1 - core)):
        scores = (
            jnp.einsum(
                "qd,kd->qk", query_rows, both[:, :HEAD_SIZE], preferred_element_type=F32
            )
            * scale
        )
        visible = (base_pos + part * half_ctx)[None, :] <= query_pos[:, None]
        scored.append((jnp.where(visible, scores, -1e30), visible, both[:, HEAD_SIZE:]))
    peak = jnp.maximum(jnp.max(scored[0][0], axis=-1), jnp.max(scored[1][0], axis=-1))
    totals, accumulated = 0.0, 0.0
    for scores, visible, value_piece in scored:
        weights = jnp.where(visible, jnp.exp(scores - peak[:, None]), 0.0)
        totals = totals + jnp.sum(weights, axis=-1)
        accumulated = accumulated + jnp.dot(
            weights.astype(BF16), value_piece, preferred_element_type=F32
        )
    attention = (
        (accumulated / totals[:, None]).reshape(rows_ctx, heads * HEAD_SIZE).astype(BF16)
    )

    hidden_z = hidden.reshape(rows, Y, Z, HEAD_SIZE).transpose(2, 0, 1, 3).reshape(Z, rows, piece)
    gates_high = gates.astype(BF16)
    gates_rest = gates - gates_high.astype(F32)
    gates_mid = gates_rest.astype(BF16)
    gates_low = (gates_rest - gates_mid.astype(F32)).astype(BF16)
    table = jnp.concatenate([routes.astype(BF16), gates_high, gates_mid, gates_low], axis=1)
    table = jnp.pad(table, ((0, 0), (0, piece - table.shape[1])))
    parcel = jnp.concatenate(
        [
            jnp.broadcast_to(attention[None], (Z, rows_ctx, piece)),
            hidden_z,
            jnp.broadcast_to(table[None], (Z, rows, piece)),
        ],
        axis=1,
    )
    parcel = swap(parcel, "z")
    attention_z = parcel[:, :rows_ctx].reshape(Z, LANES, rows, piece)
    hidden_c = parcel[:, rows_ctx : rows_ctx + rows].astype(F32)
    table_c = parcel[:, rows_ctx + rows :, : 4 * TOPK].astype(F32).reshape(Z, rows, 4, TOPK)
    routes_c = table_c[:, :, 0].astype(jnp.int32)
    gates_c = table_c[:, :, 1] + table_c[:, :, 2] + table_c[:, :, 3]

    partial = jnp.einsum("zerf,fc->ezrc", attention_z, weight_y, preferred_element_type=F32)
    projected_c = jnp.sum(swap(partial.astype(BF16), EXP).astype(F32), axis=0)
    residual_c = (hidden_c + projected_c).astype(BF16).reshape(Z * rows, piece)

    chosen, named = slots_of(routes_c)
    same = jnp.eye(Z, dtype=bool)
    pick = chosen.transpose(2, 0, 3, 1)[:, :, :, None, :] & same[None, :, None, :, None]
    pick = pick.reshape(Z * LANES * Z * MOST, Z * rows).astype(BF16)
    outbox = jnp.dot(pick, residual_c, preferred_element_type=F32).astype(BF16)
    inbox = swap(outbox.reshape(Z * LANES, Z * MOST, piece), ("z",) + EXP)
    slots = LANES * Z * MOST
    low, high = normalise(inbox, norm_gain)

    after_low = shift(low, -1)
    before_high = shift(high, 1)
    before_low = shift(low, 1)
    after_high = shift(high, -1)

    projected = swap(projected_c.astype(BF16), "z").reshape(Z, rows, Y, HEAD_SIZE)
    projected = projected.transpose(1, 2, 0, 3).reshape(rows, D)

    after_low, before_high = hand_on((after_low, before_high), (projected,))
    across_low = shift(after_low, -1)
    across_high = shift(before_high, 1)

    gate = jnp.sum(jnp.where(named, gates_c[..., None], 0.0), axis=2)
    place = jnp.where(chosen, gate[..., None], 0.0).reshape(Z, rows, Z, LANES, MOST)
    place = lax.dynamic_index_in_dim(place, lax.axis_index("z"), 2, keepdims=False)
    place = jnp.where(same[:, None, None, :, None], place[:, :, :, None, :], 0.0)
    place = place.reshape(Z * rows, slots)
    place_high = place.astype(BF16)
    place_low = (place - place_high.astype(F32)).astype(BF16)

    weights = load((w_gate[0], w_up[0], w_down[0]), (place_high, place_low))
    own_low, own_high, out_after_low, out_before_high = expert(
        (low, high, after_low, before_high), weights
    )
    out_before_low, out_after_high = expert(
        (before_low, after_high), weights, after=(own_low,)
    )
    out_across_low, out_across_high = expert(
        (across_low, across_high), weights, after=(out_before_low,)
    )
    home_low = shift(out_before_low, -1)
    home_high = shift(out_after_high, 1)
    far_low = shift(out_across_low, 1)
    far_high = shift(out_across_high, -1)
    sum_low, sum_high = add_pairs(
        (out_after_low, far_low), (out_before_high, far_high), (home_low, home_high)
    )
    sum_low, sum_high = shift(sum_low, 1), shift(sum_high, -1)
    home_low = own_low.astype(F32) + home_low.astype(F32) + sum_low.astype(F32)
    home_high = own_high.astype(F32) + home_high.astype(F32) + sum_high.astype(F32)
    returned = jnp.concatenate([home_low.astype(BF16), home_high.astype(BF16)], axis=0)

    back = swap(returned.reshape(LANES, Z * MOST, D), EXP).reshape(slots, D)
    moe_z = jnp.dot(place_high, back, preferred_element_type=F32) + jnp.dot(
        place_low, back, preferred_element_type=F32
    )
    moe = jnp.sum(swap(moe_z.astype(BF16).reshape(Z, rows, D), "z").astype(F32), axis=0)
    residual = hidden.astype(F32) + projected.astype(F32)
    attended = residual.astype(BF16)
    mixed = (residual + moe).astype(BF16)
    return (attended, mixed)


def solution(mesh):
    fine = Mesh(mesh.devices.reshape(Y, Z, X, CORE), CTX + EXP)
    every = CTX + EXP
    return jax.shard_map(
        on_device,
        mesh=fine,
        in_specs=(
            P(every, None),
            P(CTX, EXP),
            P(CTX, None),
            P(CTX, None),
            P(EXP, CTX),
            P(),
            P(every, None, None),
            P(every, None, None),
            P(every, None, None),
            P(every, None),
            P(every, None),
        ),
        out_specs=(P(every, None), P(every, None)),
        check_vma=False,
    )
```

```python
import functools

import jax
import jax.numpy as jnp
from jax import lax
from jax.experimental import pallas as pl
from jax.experimental.pallas import tpu as pltpu
from jax.sharding import Mesh
from jax.sharding import PartitionSpec as P

D = 4096
HEAD_SIZE = 128
QUERY_HEADS = 32
KEY_VALUE_HEADS = 2
TOPK = 8
MOST = 2
Y, Z, X, CORE = 4, 8, 4, 2
CTX = ("y", "z")
EXP = ("x", "core")
LANES = X * CORE
VMEM_LIMIT = 20 * 1024 * 1024
DOWN_LIMIT = 60 * 1024 * 1024
LOAD_LIMIT = 53 * 1024 * 1024
BF16 = jnp.bfloat16
F32 = jnp.float32


def spread(block, axes, count):
    return lax.all_to_all(
        jnp.broadcast_to(block[None], (count,) + block.shape), axes, 0, 0, tiled=True
    )


def swap(blocks, axes):
    return lax.all_to_all(blocks, axes, 0, 0, tiled=True)


def shift(block, step):
    return lax.ppermute(block, "y", [(i, (i + step) % Y) for i in range(Y)])


def norm_kernel(x_ref, gain_ref, low_ref, high_ref):
    lanes = LANES // 2
    rows, piece = lanes * x_ref.shape[1], x_ref.shape[2]
    for part, out_ref in enumerate((low_ref, high_ref)):

        def piece_of(i):
            x = x_ref[i * LANES + part * lanes : i * LANES + (part + 1) * lanes]
            return x.reshape(rows, piece).astype(F32)

        square = jnp.zeros((rows, 1), F32)
        for i in range(Z):
            x = piece_of(i)
            square = square + jnp.sum(x * x, axis=-1, keepdims=True)
        factor = lax.rsqrt(square * (1.0 / D) + 1e-06)
        for i in range(Z):
            x = piece_of(i) * factor
            for j in range(Y):
                at = (j * Z + i) * HEAD_SIZE
                out_ref[:, at : at + HEAD_SIZE] = (
                    x[:, j * HEAD_SIZE : (j + 1) * HEAD_SIZE] * gain_ref[:, at : at + HEAD_SIZE]
                ).astype(BF16)


def normalise(inbox, gain):
    rows = inbox.shape[0] * inbox.shape[1] // Z // 2
    return pl.pallas_call(
        norm_kernel,
        out_shape=[jax.ShapeDtypeStruct((rows, D), BF16)] * 2,
        in_specs=[pl.BlockSpec(memory_space=pltpu.VMEM)] * 2,
        out_specs=[pl.BlockSpec(memory_space=pltpu.VMEM)] * 2,
        compiler_params=pltpu.CompilerParams(vmem_limit_bytes=VMEM_LIMIT),
        cost_estimate=pl.CostEstimate(flops=6 * rows * D, bytes_accessed=8 * rows * D, transcendentals=0),
    )(inbox, gain.reshape(1, D))


STEPS = 4


def inner_kernel(count, joined, *refs):
    blocks, (gate_w, up_w) = refs[:count], refs[count : count + 2]
    x, sems = refs[-2:]
    outs = refs[-2 - count // joined : -2]
    rows = blocks[0].shape[0]
    piece = D // STEPS
    parts = [slice(i * piece, (i + 1) * piece) for i in range(STEPS)]
    copies = []
    for i, part in enumerate(parts):
        copies.append(
            [
                pltpu.make_async_copy(
                    block.at[:, part], x.at[j * rows : (j + 1) * rows, part], sems.at[i, j]
                )
                for j, block in enumerate(blocks)
            ]
        )
    for step in copies:
        for copy in step:
            copy.start()
    gate_h, up_h = 0.0, 0.0
    for i, part in enumerate(parts):
        for copy in copies[i]:
            copy.wait()
        gate_h = gate_h + jnp.dot(x[:, part], gate_w[part], preferred_element_type=F32)
        up_h = up_h + jnp.dot(x[:, part], up_w[part], preferred_element_type=F32)
    inner = (gate_h / (1.0 + jnp.exp(-gate_h)) * up_h).astype(BF16)
    for j, out_ref in enumerate(outs):
        out_ref[...] = inner[joined * j * rows : joined * (j + 1) * rows]


def inner_of(blocks, weights, joined, after=()):
    rows = blocks[0].shape[0]
    count = len(blocks)
    width = weights[0].shape[1]
    return pl.pallas_call(
        functools.partial(inner_kernel, count, joined),
        out_shape=[jax.ShapeDtypeStruct((joined * rows, width), BF16)] * (count // joined),
        in_specs=[pl.BlockSpec(memory_space=pl.ANY)] * count
        + [pl.BlockSpec(memory_space=pltpu.VMEM)] * 2
        + [pl.BlockSpec(memory_space=pl.ANY)] * len(after),
        out_specs=[pl.BlockSpec(memory_space=pltpu.VMEM)] * (count // joined),
        scratch_shapes=[
            pltpu.VMEM((count * rows, D), BF16),
            pltpu.SemaphoreType.DMA((STEPS, count)),
        ],
        compiler_params=pltpu.CompilerParams(vmem_limit_bytes=VMEM_LIMIT),
        cost_estimate=pl.CostEstimate(
            flops=4 * count * rows * D * width,
            bytes_accessed=4 * D * width + 2 * count * rows * D,
            transcendentals=count * rows * width,
        ),
    )(*blocks, *weights, *after)


def down_kernel(stored, add, *refs):
    count = len(stored)
    inners, weights = refs[:count], list(refs[count : 2 * count])
    held, sems = refs[-2:]
    results = 1 if add else count
    outs = refs[-2 - results : -2]
    copies = []
    for j in range(count):
        if not stored[j]:
            i = len(copies)
            copies.append(pltpu.make_async_copy(weights[j], held.at[i], sems.at[i]))
            weights[j] = held.at[i]
    for copy in copies:
        copy.start()
    piece = D // STEPS
    parts = [slice(i * piece, (i + 1) * piece) for i in range(STEPS)]

    def product(j, part):
        return jnp.dot(inners[j][...], weights[j][:, part], preferred_element_type=F32)

    if not add:
        for j in range(count):
            if stored[j]:
                for part in parts:
                    outs[j][:, part] = product(j, part).astype(BF16)
    for copy in copies:
        copy.wait()
    for part in parts:
        if add:
            outs[0][:, part] = sum(product(j, part) for j in range(count)).astype(BF16)
        else:
            for j in range(count):
                if not stored[j]:
                    outs[j][:, part] = product(j, part).astype(BF16)


def down(inners, weights, stored, add, after):
    count = len(inners)
    rows, width = inners[0].shape
    vmem, anywhere = pl.BlockSpec(memory_space=pltpu.VMEM), pl.BlockSpec(memory_space=pl.ANY)
    results = 1 if add else count
    return pl.pallas_call(
        functools.partial(down_kernel, stored, add),
        out_shape=[jax.ShapeDtypeStruct((rows, D), BF16)] * results,
        in_specs=[vmem] * count
        + [vmem if kept else anywhere for kept in stored]
        + [anywhere] * len(after),
        out_specs=[vmem] * results,
        scratch_shapes=[
            pltpu.VMEM((count - sum(stored), width, D), BF16),
            pltpu.SemaphoreType.DMA((count - sum(stored),)),
        ],
        compiler_params=pltpu.CompilerParams(vmem_limit_bytes=DOWN_LIMIT),
        cost_estimate=pl.CostEstimate(
            flops=2 * count * rows * D * width,
            bytes_accessed=2 * count * D * width + 8 * rows * D,
            transcendentals=0,
        ),
    )(*inners, *weights, *after)


def load_kernel(count, *refs):
    sources, targets, sems = refs[:count], refs[-1 - count : -1], refs[-1]
    copies = [
        pltpu.make_async_copy(source, target, sems.at[i])
        for i, (source, target) in enumerate(zip(sources, targets))
    ]
    for copy in copies:
        copy.start()
    for copy in copies:
        copy.wait()


def load(arrays, after):
    count = len(arrays)
    return pl.pallas_call(
        functools.partial(load_kernel, count),
        out_shape=[pltpu.VMEM(array.shape, array.dtype) for array in arrays],
        in_specs=[pl.BlockSpec(memory_space=pl.ANY)] * (count + len(after)),
        out_specs=[pl.BlockSpec(memory_space=pltpu.VMEM)] * count,
        scratch_shapes=[pltpu.SemaphoreType.DMA((count,))],
        compiler_params=pltpu.CompilerParams(vmem_limit_bytes=LOAD_LIMIT),
    )(*arrays, *after)


def hand_on_kernel(*refs):
    pass


def hand_on(blocks, after):
    count = len(blocks)
    return pl.pallas_call(
        hand_on_kernel,
        out_shape=[jax.ShapeDtypeStruct(block.shape, block.dtype) for block in blocks],
        in_specs=[pl.BlockSpec(memory_space=pl.ANY)] * (count + len(after)),
        out_specs=[pl.BlockSpec(memory_space=pl.ANY)] * count,
        input_output_aliases={i: i for i in range(count)},
    )(*blocks, *after)


def slots_of(routes):
    experts = jnp.arange(Z * LANES, dtype=jnp.int32)
    named = routes[..., None] == experts
    hit = jnp.any(named, axis=-2)
    count = hit.astype(jnp.int32)
    earlier = jnp.cumsum(count, axis=-2) - count
    chosen = hit[..., None] & (earlier[..., None] == jnp.arange(MOST, dtype=jnp.int32))
    return chosen, named


def on_device(
    hidden, queries, keys, values, out_weight, norm_gain, w_gate, w_up, w_down, routes, gates
):
    rows_ctx = queries.shape[0]
    heads = queries.shape[1] // HEAD_SIZE
    rows = routes.shape[0]
    piece = D // Z
    lane = lax.axis_index(EXP)
    ctx = lax.axis_index(CTX)
    core = lax.axis_index("core")
    scale = HEAD_SIZE ** (-0.5)

    down_own = w_down[0]
    down_after = shift(down_own, -1)
    down_before = shift(down_own, 1)

    pieces = [out_weight] + [shift(out_weight, step) for step in range(1, Y)]
    by_distance = jnp.stack(pieces[::-1] * 2)
    weight_y = lax.dynamic_slice_in_dim(by_distance, Y - 1 - lax.axis_index("y"), Y, 0)
    weight_y = weight_y.transpose(1, 0, 2).reshape(out_weight.shape[0], piece)

    head = lane * heads // (QUERY_HEADS // KEY_VALUE_HEADS)
    half_ctx = rows_ctx // CORE
    key_head = lax.dynamic_slice(keys, (core * half_ctx, head * HEAD_SIZE), (half_ctx, HEAD_SIZE))
    value_head = lax.dynamic_slice(
        values, (core * half_ctx, head * HEAD_SIZE), (half_ctx, HEAD_SIZE)
    )
    mine = spread(jnp.concatenate([key_head, value_head], axis=1), CTX, Y * Z)
    mine = mine.reshape(Y * Z * half_ctx, 2 * HEAD_SIZE)
    other = lax.ppermute(mine, "core", [(0, 1), (1, 0)])
    query_rows = queries.reshape(rows_ctx * heads, HEAD_SIZE)
    query_pos = ctx * rows_ctx + jnp.arange(rows_ctx * heads, dtype=jnp.int32) // heads
    index = jnp.arange(Y * Z * half_ctx, dtype=jnp.int32)
    base_pos = (index // half_ctx) * rows_ctx + index % half_ctx
    scored = []
    for both, part in ((mine, core), (other, 1 - core)):
        scores = (
            jnp.einsum(
                "qd,kd->qk", query_rows, both[:, :HEAD_SIZE], preferred_element_type=F32
            )
            * scale
        )
        visible = (base_pos + part * half_ctx)[None, :] <= query_pos[:, None]
        scored.append((jnp.where(visible, scores, -1e30), visible, both[:, HEAD_SIZE:]))
    peak = jnp.maximum(jnp.max(scored[0][0], axis=-1), jnp.max(scored[1][0], axis=-1))
    totals, accumulated = 0.0, 0.0
    for scores, visible, value_piece in scored:
        weights = jnp.where(visible, jnp.exp(scores - peak[:, None]), 0.0)
        totals = totals + jnp.sum(weights, axis=-1)
        accumulated = accumulated + jnp.dot(
            weights.astype(BF16), value_piece, preferred_element_type=F32
        )
    attention = (
        (accumulated / totals[:, None]).reshape(rows_ctx, heads * HEAD_SIZE).astype(BF16)
    )

    (attention,) = hand_on((attention,), pieces[1:])
    hidden_z = hidden.reshape(rows, Y, Z, HEAD_SIZE).transpose(2, 0, 1, 3).reshape(Z, rows, piece)
    gates_high = gates.astype(BF16)
    gates_rest = gates - gates_high.astype(F32)
    gates_mid = gates_rest.astype(BF16)
    gates_low = (gates_rest - gates_mid.astype(F32)).astype(BF16)
    table = jnp.concatenate([routes.astype(BF16), gates_high, gates_mid, gates_low], axis=1)
    table = jnp.pad(table, ((0, 0), (0, piece - table.shape[1])))
    parcel = jnp.concatenate(
        [
            jnp.broadcast_to(attention[None], (Z, rows_ctx, piece)),
            hidden_z,
            jnp.broadcast_to(table[None], (Z, rows, piece)),
        ],
        axis=1,
    )
    parcel = swap(parcel, "z")
    attention_z = parcel[:, :rows_ctx].reshape(Z, LANES, rows, piece)
    hidden_c = parcel[:, rows_ctx : rows_ctx + rows].astype(F32)
    table_c = parcel[:, rows_ctx + rows :, : 4 * TOPK].astype(F32).reshape(Z, rows, 4, TOPK)
    routes_c = table_c[:, :, 0].astype(jnp.int32)
    gates_c = table_c[:, :, 1] + table_c[:, :, 2] + table_c[:, :, 3]

    partial = jnp.einsum("zerf,fc->ezrc", attention_z, weight_y, preferred_element_type=F32)
    projected_c = jnp.sum(swap(partial.astype(BF16), EXP).astype(F32), axis=0)
    residual_c = (hidden_c + projected_c).astype(BF16).reshape(Z * rows, piece)

    chosen, named = slots_of(routes_c)
    same = jnp.eye(Z, dtype=bool)
    pick = chosen.transpose(2, 0, 3, 1)[:, :, :, None, :] & same[None, :, None, :, None]
    pick = pick.reshape(Z * LANES * Z * MOST, Z * rows).astype(BF16)
    outbox = jnp.dot(pick, residual_c, preferred_element_type=F32).astype(BF16)
    inbox = swap(outbox.reshape(Z * LANES, Z * MOST, piece), ("z",) + EXP)
    slots = LANES * Z * MOST
    low, high = normalise(inbox, norm_gain)
    low, high = hand_on((low, high), (down_after, down_before))

    after_low = shift(low, -1)
    before_high = shift(high, 1)
    before_low = shift(low, 1)
    after_high = shift(high, -1)

    projected = swap(projected_c.astype(BF16), "z").reshape(Z, rows, Y, HEAD_SIZE)
    projected = projected.transpose(1, 2, 0, 3).reshape(rows, D)

    after_low, before_high = hand_on((after_low, before_high), (projected,))
    across_low = shift(after_low, -1)
    across_high = shift(before_high, 1)

    gate = jnp.sum(jnp.where(named, gates_c[..., None], 0.0), axis=2)
    place = jnp.where(chosen, gate[..., None], 0.0).reshape(Z, rows, Z, LANES, MOST)
    place = lax.dynamic_index_in_dim(place, lax.axis_index("z"), 2, keepdims=False)
    place = jnp.where(same[:, None, None, :, None], place[:, :, :, None, :], 0.0)
    place = place.reshape(Z * rows, slots)
    place_high = place.astype(BF16)
    place_low = (place - place_high.astype(F32)).astype(BF16)

    gate_w, up_w, after_w = load(
        (w_gate[0], w_up[0], down_after), (place_high, place_low, down_before)
    )
    inner_own, inner_after, inner_before = inner_of(
        (low, high, after_low, after_high, before_low, before_high), (gate_w, up_w), 2
    )
    inner_low, inner_high = inner_of(
        (across_low, across_high), (gate_w, up_w), 1, after=(inner_own,)
    )
    from_after = shift(inner_before, -1)
    from_before = shift(inner_after, 1)
    relay_low, relay_high = down(
        (shift(inner_low, 1), shift(inner_high, -1)),
        (down_before, after_w),
        (False, True),
        False,
        (from_after, from_before),
    )
    far = jnp.concatenate([shift(relay_low, 1), shift(relay_high, -1)], axis=0)
    (near,) = down(
        (inner_own, from_after, from_before),
        (down_own, after_w, down_before),
        (False, True, False),
        True,
        (relay_low,),
    )
    returned = (near.astype(F32) + far.astype(F32)).astype(BF16)

    back = swap(returned.reshape(LANES, Z * MOST, D), EXP).reshape(slots, D)
    moe_z = jnp.dot(place_high, back, preferred_element_type=F32) + jnp.dot(
        place_low, back, preferred_element_type=F32
    )
    moe = jnp.sum(swap(moe_z.astype(BF16).reshape(Z, rows, D), "z").astype(F32), axis=0)
    residual = hidden.astype(F32) + projected.astype(F32)
    attended = residual.astype(BF16)
    mixed = (residual + moe).astype(BF16)
    return (attended, mixed)


def solution(mesh):
    fine = Mesh(mesh.devices.reshape(Y, Z, X, CORE), CTX + EXP)
    every = CTX + EXP
    return jax.shard_map(
        on_device,
        mesh=fine,
        in_specs=(
            P(every, None),
            P(CTX, EXP),
            P(CTX, None),
            P(CTX, None),
            P(EXP, CTX),
            P(),
            P(every, None, None),
            P(every, None, None),
            P(every, None, None),
            P(every, None),
            P(every, None),
        ),
        out_specs=(P(every, None), P(every, None)),
        check_vma=False,
    )
```

```python
import functools

import jax
import jax.numpy as jnp
from jax import lax
from jax.experimental import pallas as pl
from jax.experimental.pallas import tpu as pltpu
from jax.sharding import Mesh
from jax.sharding import PartitionSpec as P

D = 4096
HEAD_SIZE = 128
QUERY_HEADS = 32
KEY_VALUE_HEADS = 2
TOPK = 8
MOST = 2
Y, Z, X, CORE = 4, 8, 4, 2
CTX = ("y", "z")
EXP = ("x", "core")
LANES = X * CORE
VMEM_LIMIT = 20 * 1024 * 1024
DOWN_LIMIT = 60 * 1024 * 1024
LOAD_LIMIT = 53 * 1024 * 1024
BF16 = jnp.bfloat16
F32 = jnp.float32


def spread(block, axes, count):
    return lax.all_to_all(
        jnp.broadcast_to(block[None], (count,) + block.shape), axes, 0, 0, tiled=True
    )


def swap(blocks, axes):
    return lax.all_to_all(blocks, axes, 0, 0, tiled=True)


def shift(block, step):
    return lax.ppermute(block, "y", [(i, (i + step) % Y) for i in range(Y)])


def norm_kernel(x_ref, gain_ref, low_ref, high_ref):
    lanes = LANES // 2
    rows, piece = lanes * x_ref.shape[1], x_ref.shape[2]
    for part, out_ref in enumerate((low_ref, high_ref)):

        def piece_of(i):
            x = x_ref[i * LANES + part * lanes : i * LANES + (part + 1) * lanes]
            return x.reshape(rows, piece).astype(F32)

        square = jnp.zeros((rows, 1), F32)
        for i in range(Z):
            x = piece_of(i)
            square = square + jnp.sum(x * x, axis=-1, keepdims=True)
        factor = lax.rsqrt(square * (1.0 / D) + 1e-06)
        for i in range(Z):
            x = piece_of(i) * factor
            for j in range(Y):
                at = (j * Z + i) * HEAD_SIZE
                out_ref[:, at : at + HEAD_SIZE] = (
                    x[:, j * HEAD_SIZE : (j + 1) * HEAD_SIZE] * gain_ref[:, at : at + HEAD_SIZE]
                ).astype(BF16)


def normalise(inbox, gain):
    rows = inbox.shape[0] * inbox.shape[1] // Z // 2
    return pl.pallas_call(
        norm_kernel,
        out_shape=[jax.ShapeDtypeStruct((rows, D), BF16)] * 2,
        in_specs=[pl.BlockSpec(memory_space=pltpu.VMEM)] * 2,
        out_specs=[pl.BlockSpec(memory_space=pltpu.VMEM)] * 2,
        compiler_params=pltpu.CompilerParams(vmem_limit_bytes=VMEM_LIMIT),
        cost_estimate=pl.CostEstimate(flops=6 * rows * D, bytes_accessed=8 * rows * D, transcendentals=0),
    )(inbox, gain.reshape(1, D))


STEPS = 4


def inner_kernel(count, joined, *refs):
    blocks, (gate_w, up_w) = refs[:count], refs[count : count + 2]
    x, sems = refs[-2:]
    outs = refs[-2 - count // joined : -2]
    rows = blocks[0].shape[0]
    piece = D // STEPS
    parts = [slice(i * piece, (i + 1) * piece) for i in range(STEPS)]
    copies = []
    for i, part in enumerate(parts):
        copies.append(
            [
                pltpu.make_async_copy(
                    block.at[:, part], x.at[j * rows : (j + 1) * rows, part], sems.at[i, j]
                )
                for j, block in enumerate(blocks)
            ]
        )
    for step in copies:
        for copy in step:
            copy.start()
    gate_h, up_h = 0.0, 0.0
    for i, part in enumerate(parts):
        for copy in copies[i]:
            copy.wait()
        gate_h = gate_h + jnp.dot(x[:, part], gate_w[part], preferred_element_type=F32)
        up_h = up_h + jnp.dot(x[:, part], up_w[part], preferred_element_type=F32)
    inner = (gate_h / (1.0 + jnp.exp(-gate_h)) * up_h).astype(BF16)
    for j, out_ref in enumerate(outs):
        out_ref[...] = inner[joined * j * rows : joined * (j + 1) * rows]


def inner_of(blocks, weights, joined, after=()):
    rows = blocks[0].shape[0]
    count = len(blocks)
    width = weights[0].shape[1]
    return pl.pallas_call(
        functools.partial(inner_kernel, count, joined),
        out_shape=[jax.ShapeDtypeStruct((joined * rows, width), BF16)] * (count // joined),
        in_specs=[pl.BlockSpec(memory_space=pl.ANY)] * count
        + [pl.BlockSpec(memory_space=pltpu.VMEM)] * 2
        + [pl.BlockSpec(memory_space=pl.ANY)] * len(after),
        out_specs=[pl.BlockSpec(memory_space=pltpu.VMEM)] * (count // joined),
        scratch_shapes=[
            pltpu.VMEM((count * rows, D), BF16),
            pltpu.SemaphoreType.DMA((STEPS, count)),
        ],
        compiler_params=pltpu.CompilerParams(vmem_limit_bytes=VMEM_LIMIT),
        cost_estimate=pl.CostEstimate(
            flops=4 * count * rows * D * width,
            bytes_accessed=4 * D * width + 2 * count * rows * D,
            transcendentals=count * rows * width,
        ),
    )(*blocks, *weights, *after)


def down_kernel(stored, add, *refs):
    count = len(stored)
    inners, weights = refs[:count], list(refs[count : 2 * count])
    held, sems = refs[-2:]
    results = 1 if add else count
    outs = refs[-2 - results : -2]
    copies = []
    for j in range(count):
        if not stored[j]:
            i = len(copies)
            copies.append(pltpu.make_async_copy(weights[j], held.at[i], sems.at[i]))
            weights[j] = held.at[i]
    for copy in copies:
        copy.start()
    piece = D // STEPS
    parts = [slice(i * piece, (i + 1) * piece) for i in range(STEPS)]

    def product(j, part):
        return jnp.dot(inners[j][...], weights[j][:, part], preferred_element_type=F32)

    if not add:
        for j in range(count):
            if stored[j]:
                for part in parts:
                    outs[j][:, part] = product(j, part).astype(BF16)
    for copy in copies:
        copy.wait()
    for part in parts:
        if add:
            outs[0][:, part] = sum(product(j, part) for j in range(count)).astype(BF16)
        else:
            for j in range(count):
                if not stored[j]:
                    outs[j][:, part] = product(j, part).astype(BF16)


def down(inners, weights, stored, add, after):
    count = len(inners)
    rows, width = inners[0].shape
    vmem, anywhere = pl.BlockSpec(memory_space=pltpu.VMEM), pl.BlockSpec(memory_space=pl.ANY)
    results = 1 if add else count
    return pl.pallas_call(
        functools.partial(down_kernel, stored, add),
        out_shape=[jax.ShapeDtypeStruct((rows, D), BF16)] * results,
        in_specs=[vmem] * count
        + [vmem if kept else anywhere for kept in stored]
        + [anywhere] * len(after),
        out_specs=[vmem] * results,
        scratch_shapes=[
            pltpu.VMEM((count - sum(stored), width, D), BF16),
            pltpu.SemaphoreType.DMA((count - sum(stored),)),
        ],
        compiler_params=pltpu.CompilerParams(vmem_limit_bytes=DOWN_LIMIT),
        cost_estimate=pl.CostEstimate(
            flops=2 * count * rows * D * width,
            bytes_accessed=2 * count * D * width + 8 * rows * D,
            transcendentals=0,
        ),
    )(*inners, *weights, *after)


def load_kernel(count, *refs):
    sources, targets, sems = refs[:count], refs[-1 - count : -1], refs[-1]
    copies = [
        pltpu.make_async_copy(source, target, sems.at[i])
        for i, (source, target) in enumerate(zip(sources, targets))
    ]
    for copy in copies:
        copy.start()
    for copy in copies:
        copy.wait()


def load(arrays, after):
    count = len(arrays)
    return pl.pallas_call(
        functools.partial(load_kernel, count),
        out_shape=[pltpu.VMEM(array.shape, array.dtype) for array in arrays],
        in_specs=[pl.BlockSpec(memory_space=pl.ANY)] * (count + len(after)),
        out_specs=[pl.BlockSpec(memory_space=pltpu.VMEM)] * count,
        scratch_shapes=[pltpu.SemaphoreType.DMA((count,))],
        compiler_params=pltpu.CompilerParams(vmem_limit_bytes=LOAD_LIMIT),
    )(*arrays, *after)


def hand_on_kernel(*refs):
    pass


def hand_on(blocks, after):
    count = len(blocks)
    return pl.pallas_call(
        hand_on_kernel,
        out_shape=[jax.ShapeDtypeStruct(block.shape, block.dtype) for block in blocks],
        in_specs=[pl.BlockSpec(memory_space=pl.ANY)] * (count + len(after)),
        out_specs=[pl.BlockSpec(memory_space=pl.ANY)] * count,
        input_output_aliases={i: i for i in range(count)},
    )(*blocks, *after)


def slots_of(routes):
    experts = jnp.arange(Z * LANES, dtype=jnp.int32)
    named = routes[..., None] == experts
    hit = jnp.any(named, axis=-2)
    count = hit.astype(jnp.int32)
    earlier = jnp.cumsum(count, axis=-2) - count
    chosen = hit[..., None] & (earlier[..., None] == jnp.arange(MOST, dtype=jnp.int32))
    return chosen, named


def on_device(
    hidden, queries, keys, values, out_weight, norm_gain, w_gate, w_up, w_down, routes, gates
):
    rows_ctx = queries.shape[0]
    heads = queries.shape[1] // HEAD_SIZE
    rows = routes.shape[0]
    piece = D // Z
    lane = lax.axis_index(EXP)
    ctx = lax.axis_index(CTX)
    core = lax.axis_index("core")
    scale = HEAD_SIZE ** (-0.5)

    down_own = w_down[0]
    down_after = shift(down_own, -1)
    down_before = shift(down_own, 1)

    pieces = [out_weight] + [shift(out_weight, step) for step in range(1, Y)]
    by_distance = jnp.stack(pieces[::-1] * 2)
    weight_y = lax.dynamic_slice_in_dim(by_distance, Y - 1 - lax.axis_index("y"), Y, 0)
    weight_y = weight_y.transpose(1, 0, 2).reshape(out_weight.shape[0], piece)

    head = lane * heads // (QUERY_HEADS // KEY_VALUE_HEADS)
    half_ctx = rows_ctx // CORE
    key_head = lax.dynamic_slice(keys, (core * half_ctx, head * HEAD_SIZE), (half_ctx, HEAD_SIZE))
    value_head = lax.dynamic_slice(
        values, (core * half_ctx, head * HEAD_SIZE), (half_ctx, HEAD_SIZE)
    )
    mine = spread(jnp.concatenate([key_head, value_head], axis=1), CTX, Y * Z)
    mine = mine.reshape(Y * Z * half_ctx, 2 * HEAD_SIZE)
    other = lax.ppermute(mine, "core", [(0, 1), (1, 0)])
    query_rows = queries.reshape(rows_ctx * heads, HEAD_SIZE)
    query_pos = ctx * rows_ctx + jnp.arange(rows_ctx * heads, dtype=jnp.int32) // heads
    index = jnp.arange(Y * Z * half_ctx, dtype=jnp.int32)
    base_pos = (index // half_ctx) * rows_ctx + index % half_ctx
    scored = []
    for both, part in ((mine, core), (other, 1 - core)):
        scores = (
            jnp.einsum(
                "qd,kd->qk", query_rows, both[:, :HEAD_SIZE], preferred_element_type=F32
            )
            * scale
        )
        visible = (base_pos + part * half_ctx)[None, :] <= query_pos[:, None]
        scored.append((jnp.where(visible, scores, -1e30), visible, both[:, HEAD_SIZE:]))
    peak = jnp.maximum(jnp.max(scored[0][0], axis=-1), jnp.max(scored[1][0], axis=-1))
    totals, accumulated = 0.0, 0.0
    for scores, visible, value_piece in scored:
        weights = jnp.where(visible, jnp.exp(scores - peak[:, None]), 0.0)
        totals = totals + jnp.sum(weights, axis=-1)
        accumulated = accumulated + jnp.dot(
            weights.astype(BF16), value_piece, preferred_element_type=F32
        )
    attention = (
        (accumulated / totals[:, None]).reshape(rows_ctx, heads * HEAD_SIZE).astype(BF16)
    )

    hidden_z = hidden.reshape(rows, Y, Z, HEAD_SIZE).transpose(2, 0, 1, 3).reshape(Z, rows, piece)
    gates_high = gates.astype(BF16)
    gates_rest = gates - gates_high.astype(F32)
    gates_mid = gates_rest.astype(BF16)
    gates_low = (gates_rest - gates_mid.astype(F32)).astype(BF16)
    table = jnp.concatenate([routes.astype(BF16), gates_high, gates_mid, gates_low], axis=1)
    table = jnp.pad(table, ((0, 0), (0, piece - table.shape[1])))
    parcel = jnp.concatenate(
        [
            jnp.broadcast_to(attention[None], (Z, rows_ctx, piece)),
            hidden_z,
            jnp.broadcast_to(table[None], (Z, rows, piece)),
        ],
        axis=1,
    )
    (parcel,) = hand_on((parcel,), pieces[1:])
    parcel = swap(parcel, "z")
    attention_z = parcel[:, :rows_ctx].reshape(Z, LANES, rows, piece)
    hidden_c = parcel[:, rows_ctx : rows_ctx + rows].astype(F32)
    table_c = parcel[:, rows_ctx + rows :, : 4 * TOPK].astype(F32).reshape(Z, rows, 4, TOPK)
    routes_c = table_c[:, :, 0].astype(jnp.int32)
    gates_c = table_c[:, :, 1] + table_c[:, :, 2] + table_c[:, :, 3]

    partial = jnp.einsum("zerf,fc->ezrc", attention_z, weight_y, preferred_element_type=F32)
    projected_c = jnp.sum(swap(partial.astype(BF16), EXP).astype(F32), axis=0)
    residual_c = (hidden_c + projected_c).astype(BF16).reshape(Z * rows, piece)

    chosen, named = slots_of(routes_c)
    same = jnp.eye(Z, dtype=bool)
    pick = chosen.transpose(2, 0, 3, 1)[:, :, :, None, :] & same[None, :, None, :, None]
    pick = pick.reshape(Z * LANES * Z * MOST, Z * rows).astype(BF16)
    outbox = jnp.dot(pick, residual_c, preferred_element_type=F32).astype(BF16)
    inbox = swap(outbox.reshape(Z * LANES, Z * MOST, piece), ("z",) + EXP)
    slots = LANES * Z * MOST
    low, high = normalise(inbox, norm_gain)
    low, high = hand_on((low, high), (down_after, down_before))

    after_low = shift(low, -1)
    before_high = shift(high, 1)
    before_low = shift(low, 1)
    after_high = shift(high, -1)

    projected = swap(projected_c.astype(BF16), "z").reshape(Z, rows, Y, HEAD_SIZE)
    projected = projected.transpose(1, 2, 0, 3).reshape(rows, D)

    after_low, before_high = hand_on((after_low, before_high), (projected,))
    across_low = shift(after_low, -1)
    across_high = shift(before_high, 1)

    gate = jnp.sum(jnp.where(named, gates_c[..., None], 0.0), axis=2)
    place = jnp.where(chosen, gate[..., None], 0.0).reshape(Z, rows, Z, LANES, MOST)
    place = lax.dynamic_index_in_dim(place, lax.axis_index("z"), 2, keepdims=False)
    place = jnp.where(same[:, None, None, :, None], place[:, :, :, None, :], 0.0)
    place = place.reshape(Z * rows, slots)
    place_high = place.astype(BF16)
    place_low = (place - place_high.astype(F32)).astype(BF16)

    gate_w, up_w, after_w = load(
        (w_gate[0], w_up[0], down_after), (place_high, place_low, down_before)
    )
    inner_own, inner_after, inner_before = inner_of(
        (low, high, after_low, after_high, before_low, before_high), (gate_w, up_w), 2
    )
    inner_low, inner_high = inner_of(
        (across_low, across_high), (gate_w, up_w), 1, after=(inner_own,)
    )
    from_after = shift(inner_before, -1)
    from_before = shift(inner_after, 1)
    relay_low, relay_high = down(
        (shift(inner_low, 1), shift(inner_high, -1)),
        (down_before, after_w),
        (False, True),
        False,
        (from_after, from_before),
    )
    far = jnp.concatenate([shift(relay_low, 1), shift(relay_high, -1)], axis=0)
    (near,) = down(
        (inner_own, from_after, from_before),
        (down_own, after_w, down_before),
        (False, True, False),
        True,
        (relay_low,),
    )
    returned = (near.astype(F32) + far.astype(F32)).astype(BF16)

    back = swap(returned.reshape(LANES, Z * MOST, D), EXP).reshape(slots, D)
    moe_z = jnp.dot(place_high, back, preferred_element_type=F32) + jnp.dot(
        place_low, back, preferred_element_type=F32
    )
    moe = jnp.sum(swap(moe_z.astype(BF16).reshape(Z, rows, D), "z").astype(F32), axis=0)
    residual = hidden.astype(F32) + projected.astype(F32)
    attended = residual.astype(BF16)
    mixed = (residual + moe).astype(BF16)
    return (attended, mixed)


def solution(mesh):
    fine = Mesh(mesh.devices.reshape(Y, Z, X, CORE), CTX + EXP)
    every = CTX + EXP
    return jax.shard_map(
        on_device,
        mesh=fine,
        in_specs=(
            P(every, None),
            P(CTX, EXP),
            P(CTX, None),
            P(CTX, None),
            P(EXP, CTX),
            P(),
            P(every, None, None),
            P(every, None, None),
            P(every, None, None),
            P(every, None),
            P(every, None),
        ),
        out_specs=(P(every, None), P(every, None)),
        check_vma=False,
    )
```
